512 devices in a mesh: tm: 32 (over y_hi, z, core), rows: 16 (over x, y_lo).
Axes of the slice: x: 4, y: 8 (y_hi: 2, y_lo: 4; y = y_hi * 4 + y_lo), z: 8, core: 2. Of those that a mesh axis runs over, the one named last changes fastest.
Arguments:
- col_feat: bfloat16 [32, 256, 256], P('tm', 'rows'), may hold values from -6 to 6
- w_depth: bfloat16 [256, 128], replicated, may hold values from -0.375 to 0.375
- w_ctx: bfloat16 [256, 80], replicated, may hold values from -0.375 to 0.375
- col_table: int32 [128, 128], P('rows'), may hold values from 0 to 255
- w_bev: bfloat16 [3, 3, 80, 80], replicated, may hold values from -0.21875 to 0.21875
- offsets: int32 [32, 16, 2], P('tm'), may hold values from -4 to 4, as said below
- w_join: bfloat16 [3, 3, 1360, 160], replicated, may hold values from -0.0546875 to 0.0546875
- w_out: bfloat16 [3, 3, 160, 160], replicated, may hold values from -0.15625 to 0.15625
Outputs:
- joined: bfloat16 [32, 128, 160, 128], P('tm', 'rows')
The draws below stay inside these ranges and needn't reach their ends.
Inputs may be any that keep to these rules, and one draw needn't show every extreme that they name: Where f - k >= 0, offsets[f, k - 1, :] is the ego path's displacement from frame f to frame f - k: the sum of k per-frame steps of -1, 0 or 1 in each coordinate, clipped to the range.
All inputs are finite; a program needn't handle non-finite values.
Results may differ from the reference program's by a relative error of at most 0.0065.
Values may be sent and summed in bfloat16 or wider, within the bound.
No kernel may reach another device: no remote copies, remote signals or barrier semaphores. Data moves between devices by JAX's collectives and lax.ppermute only.
A program may use at most 128 MiB of HBM per device.

```python
import jax
import jax.numpy as jnp
from jax import lax

C = 80
C2 = 160
K = 256
NCOL = 256
W = 128
PREV = 16
H = 128
FRAMES = 32


def draw_offsets(key, part):
    key = jax.random.fold_in(key, 7)
    steps_taken = jax.random.randint(key, (FRAMES, 2), -1, 2).astype(jnp.int32)
    frame_ids = jnp.arange(FRAMES, dtype=jnp.int32)
    forced = (frame_ids >= 1) & (frame_ids <= 4)
    pushed = jnp.array([1, -1], jnp.int32)[None, :]
    steps_taken = jnp.where(forced[:, None], pushed, steps_taken)
    travel = jnp.cumsum(steps_taken, axis=0).astype(jnp.int32)
    lookback = jnp.arange(1, PREV + 1, dtype=jnp.int32)
    earlier_ids = jnp.maximum(frame_ids[:, None] - lookback[None, :], 0)
    moved = travel[earlier_ids] - travel[frame_ids][:, None, :]
    return jnp.clip(moved, -4, 4).astype(jnp.int32)


def touch_ends(entries, rng, low, high):
    dims = entries.shape
    index_at = [jax.random.randint(jax.random.fold_in(rng, axis), (), 0, dims[axis]) for axis in range(len(dims))]
    entries = entries.at[tuple(index_at)].set(low)
    longest = dims.index(max(dims))
    index_at[longest] = (index_at[longest] + 1) % dims[longest]
    return entries.at[tuple(index_at)].set(high)


def steps_of(rng, extent, cuts, least, top_value):
    loudness, own = 1.0, jax.random.fold_in(rng, 6)
    for dim, parts in cuts:
        heights = jnp.exp(jax.random.uniform(jax.random.fold_in(own, dim), (parts,), jnp.float32, least / len(cuts), top_value / len(cuts)))
        loudness = loudness * jnp.repeat(heights, extent[dim] // parts).reshape([-1 if axis == dim else 1 for axis in range(len(extent))])
    return loudness


def noise(key, dims, width, bound, shards=(), kind=jnp.bfloat16):
    gain = steps_of(key, dims, shards, -0.22, 0.18) if shards else 1.0
    drawn = jax.random.normal(key, dims, jnp.float32) * width * gain
    return jnp.minimum(jnp.maximum(drawn, -bound), bound).astype(kind)


def setup_inputs(seed: int = 0) -> dict:
    keys = jax.random.split(jax.random.key(seed), 9)
    return {
        "col_feat": noise(keys[0], (FRAMES, NCOL, K), 1.0, 6.0, ((0, 32), (1, 16))),
        "w_depth": noise(keys[1], (K, H), K ** -0.5, 0.375),
        "w_ctx": noise(keys[2], (K, C), K ** -0.5, 0.375),
        "col_table": touch_ends(jax.random.randint(keys[3], (H, W), 0, NCOL), jax.random.fold_in(keys[3], 1), 0, NCOL - 1).astype(jnp.int32),
        "w_bev": noise(keys[4], (3, 3, C, C), (9 * C) ** -0.5, 0.21875),
        "offsets": draw_offsets(jax.random.fold_in(keys[8], 71), 0),
        "w_join": noise(keys[6], (3, 3, (PREV + 1) * C, C2), (9 * (PREV + 1) * C) ** -0.5, 0.0546875),
        "w_out": noise(keys[7], (3, 3, C2, C2), (9 * C2) ** -0.5, 0.15625),
    }


def conv_plain(field, weight):
    rows = field.shape[0]
    cols = field.shape[2]
    padded = jnp.pad(field.astype(jnp.float32), ((1, 1), (0, 0), (1, 1)))
    weight = weight.astype(jnp.float32)
    total = jnp.zeros((rows, weight.shape[3], cols), jnp.float32)
    for a in range(3):
        for b in range(3):
            total = total + jnp.einsum("rcw,co->row", padded[a:a + rows, :, b:b + cols], weight[a, b])
    return total


def reference(col_feat, w_depth, w_ctx, col_table, w_bev, offsets, w_join, w_out):
    feats = col_feat.astype(jnp.float32)
    depth = jax.nn.sigmoid(jnp.einsum("fnk,kd->fnd", feats, w_depth.astype(jnp.float32)))
    ctx = jnp.einsum("fnk,kc->fnc", feats, w_ctx.astype(jnp.float32))
    ray = (depth[:, :, :, None] * ctx[:, :, None, :]).astype(jnp.bfloat16)
    rows_iota = jnp.arange(H, dtype=jnp.int32)[:, None]
    lifted = jnp.transpose(ray[:, col_table, rows_iota, :], (0, 1, 3, 2))

    def lift_conv(field):
        return jax.nn.silu(conv_plain(field, w_bev)).astype(jnp.bfloat16)

    bev = lax.map(lift_conv, lifted)
    padded = jnp.pad(bev, ((PREV, 0), (5, 5), (0, 0), (4, 4)))
    zero_moves = jnp.zeros((FRAMES, 1, 2), jnp.int32)
    moves_all = jnp.concatenate([zero_moves, offsets.astype(jnp.int32)], axis=1)
    w_win = w_join.astype(jnp.float32).reshape(3, 3, PREV + 1, C, C2)
    anchor = jnp.zeros((), jnp.int32)

    def warp(slab, move):
        return lax.dynamic_slice(slab, (4 + move[0], anchor, 4 + move[1]), (H + 2, C, W))

    def one_frame(frame):
        window = lax.dynamic_slice_in_dim(padded, frame, PREV + 1, 0)[::-1]
        warped = jax.vmap(warp)(window, moves_all[frame]).astype(jnp.float32)
        wide = jnp.pad(warped, ((0, 0), (0, 0), (0, 0), (1, 1)))
        total = jnp.zeros((H, C2, W), jnp.float32)
        for a in range(3):
            for b in range(3):
                total = total + jnp.einsum("krcw,kco->row", wide[:, a:a + H, :, b:b + W], w_win[a, b])
        hidden = jax.nn.silu(total).astype(jnp.bfloat16)
        return conv_plain(hidden, w_out).astype(jnp.bfloat16)

    return lax.map(one_frame, jnp.arange(FRAMES, dtype=jnp.int32))
```

```python
import functools

import jax
import jax.numpy as jnp
from jax import lax
from jax.experimental import pallas as pl
from jax.experimental.pallas import tpu as pltpu
from jax.sharding import PartitionSpec as P

BF = jnp.bfloat16
F32 = jnp.float32
EXTRA = 7
REACH = 4


def silu(v):
    return v / (1.0 + jnp.exp(-v))


def spread(acc, lane, chans):
    cols = acc.shape[1]
    low = jnp.where(lane == 0, 0.0, pltpu.roll(acc[:chans], 1, 1))
    high = jnp.where(lane == cols - 1, 0.0, pltpu.roll(acc[2 * chans :], cols - 1, 1))
    return acc[chans : 2 * chans] + low + high


def pack_kernel(shape, scal, feats, w_depth, w_ctx, table, out, stack):
    blocks, frames, columns, chans, rows, total = shape
    frame = scal[1]
    for slot in range(frames):
        source = frame - (frames - 1) + slot
        piece = feats[jnp.maximum(source, 0)]
        stack[slot * columns : (slot + 1) * columns, :] = jnp.where(
            source >= 0, piece, jnp.zeros_like(piece)
        )
    stacked = stack[...]
    depth = jax.nn.sigmoid(jnp.dot(stacked, w_depth[...], preferred_element_type=F32))
    ctx = jnp.dot(stacked, w_ctx[...], preferred_element_type=F32)
    lane = lax.broadcasted_iota(jnp.int32, ctx.shape, 1)
    tab = jnp.concatenate([table[...].astype(F32), jnp.zeros_like(table[...]).astype(F32)], axis=0)
    for block in range(blocks):
        first = rows * block - EXTRA
        turned = pltpu.roll(depth, (chans - first) % depth.shape[1], 1)
        low = max(chans, chans - first)
        high = min(chans + rows + 2 * EXTRA, total - first + chans)
        keep = (lane >= low) & (lane < high)
        message = jnp.where(lane < chans, ctx, jnp.where(keep, turned, 0.0))
        out[block, : frames * columns, :] = message.astype(BF)
        out[block, frames * columns :, :] = tab.astype(BF)


def main_kernel(shape, scal, got, w_bev, w_join, w_out, out, ctx, dep, tab, lifted, moved, hidden):
    blocks, frames, columns, chans, rows, total, cols, wide = shape
    here = scal[0]
    count = blocks * columns
    span = rows + 2 * EXTRA

    for k in range(frames):
        slot = frames - 1 - k
        piece = got[:, slot * columns : (slot + 1) * columns, :].reshape(count, cols)
        turned = piece.astype(F32).T
        ctx[k * chans : (k + 1) * chans, :] = turned[:chans].astype(BF)
        dep[:, k, :] = turned[chans : chans + span]
    for side in range(3):
        block = jnp.clip(here + (side - 1), 0, blocks - 1)
        both = got[block, frames * columns :, :].astype(F32)
        tab[side * rows : (side + 1) * rows, :] = both[:rows]

    number = lax.broadcasted_iota(jnp.int32, (count, cols), 0)

    def lift(pair, carry):
        hots = []
        gains = []
        for half in range(2):
            row = 2 * pair + half
            seen = tab[pl.ds(row + rows - EXTRA, 1), :].astype(jnp.int32)
            hot = jnp.where(number == seen, 1.0, 0.0).astype(BF)
            hots.append(hot)
            gains.append(jnp.dot(dep[row].astype(BF), hot, preferred_element_type=F32))
        hot = jnp.concatenate(hots, axis=1)
        group = 4
        for start in range(0, frames, group):
            stop = min(start + group, frames)
            picked = jnp.dot(
                ctx[start * chans : stop * chans, :], hot, preferred_element_type=F32
            )
            for k in range(start, stop):
                part = picked[(k - start) * chans : (k - start + 1) * chans]
                for half in range(2):
                    value = part[:, half * cols : (half + 1) * cols] * gains[half][k : k + 1, :]
                    lifted[2 * pair + half, k * chans : (k + 1) * chans, :] = value.astype(BF)
        return carry

    lax.fori_loop(0, span // 2, lift, 0)

    lane = lax.broadcasted_iota(jnp.int32, (chans, cols), 1)
    need = rows + 4

    def bev(k, carry):
        dy = scal[2 + 2 * k]
        dx = scal[3 + 2 * k]
        base = dy + REACH
        at = pl.multiple_of(k * chans, 16)
        inside = (lane + dx >= 0) & (lane + dx < cols)
        turn = jnp.where(dx > 0, cols - dx, -dx)
        for pair in range(need // 2):
            sides = [
                lifted[pl.ds(base + 2 * pair + half, 3), pl.ds(at, chans), :].reshape(3 * chans, cols)
                for half in range(2)
            ]
            acc = jnp.dot(w_bev[...], jnp.concatenate(sides, axis=1), preferred_element_type=F32)
            for half in range(2):
                row = here * rows - 2 + dy + 2 * pair + half
                value = silu(spread(acc[:, half * cols : (half + 1) * cols], lane, chans))
                value = pltpu.roll(value, turn, 1)
                keep = inside & (row >= 0) & (row < total)
                moved[2 * pair + half, pl.ds(at, chans), :] = jnp.where(keep, value, 0.0).astype(BF)
        return carry

    lax.fori_loop(0, frames, bev, 0)

    lane_wide = lax.broadcasted_iota(jnp.int32, (wide, cols), 1)

    def join(pair, carry):
        sides = [
            moved[pl.ds(2 * pair + half, 3), :, :].reshape(3 * frames * chans, cols) for half in range(2)
        ]
        acc = jnp.dot(w_join[...], jnp.concatenate(sides, axis=1), preferred_element_type=F32)
        for half in range(2):
            row = here * rows - 1 + 2 * pair + half
            value = silu(spread(acc[:, half * cols : (half + 1) * cols], lane_wide, wide))
            keep = (row >= 0) & (row < total)
            hidden[2 * pair + half] = jnp.where(keep, value, 0.0).astype(BF)
        return carry

    lax.fori_loop(0, (rows + 2) // 2, join, 0)

    def close(pair, carry):
        sides = [hidden[pl.ds(2 * pair + half, 3), :, :].reshape(3 * wide, cols) for half in range(2)]
        acc = jnp.dot(w_out[...], jnp.concatenate(sides, axis=1), preferred_element_type=F32)
        for half in range(2):
            value = spread(acc[:, half * cols : (half + 1) * cols], lane_wide, wide)
            out[2 * pair + half] = value.astype(BF)
        return carry

    lax.fori_loop(0, rows // 2, close, 0)


def taps(weight):
    turned = jnp.transpose(weight, (1, 3, 0, 2))
    return turned.reshape(weight.shape[1] * weight.shape[3], weight.shape[0] * weight.shape[2])


def shards(col_feat, w_depth, w_ctx, col_table, w_bev, offsets, w_join, w_out):
    rows, cols = col_table.shape
    frames = offsets.shape[1] + 1
    chans = w_ctx.shape[1]
    wide = w_out.shape[3]
    columns, depth_k = col_feat.shape[1:]
    blocks = lax.axis_size("rows")
    window = lax.axis_size("tm")
    total = w_depth.shape[1]
    span = rows + 2 * EXTRA

    feats = jnp.broadcast_to(col_feat, (window, columns, depth_k))
    feats = lax.all_to_all(feats, "tm", split_axis=0, concat_axis=0, tiled=True)

    moves = jnp.concatenate([jnp.zeros((1, 2), jnp.int32), offsets[0]], axis=0)
    scal = jnp.concatenate(
        [
            lax.axis_index("rows").astype(jnp.int32).reshape(1),
            lax.axis_index("tm").astype(jnp.int32).reshape(1),
            moves.reshape(-1),
        ]
    )
    vmem = pl.BlockSpec(memory_space=pltpu.VMEM)
    smem = pl.BlockSpec(memory_space=pltpu.SMEM)
    deep = frames * columns + 2 * rows
    messages = pl.pallas_call(
        functools.partial(pack_kernel, (blocks, frames, columns, chans, rows, total)),
        out_shape=jax.ShapeDtypeStruct((blocks, deep, cols), BF),
        in_specs=[smem, vmem, vmem, vmem, vmem],
        out_specs=vmem,
        scratch_shapes=[pltpu.VMEM((frames * columns, depth_k), BF)],
        compiler_params=pltpu.CompilerParams(vmem_limit_bytes=32 * 1024 * 1024),
        name="pack",
    )(scal, feats, w_depth, jnp.pad(w_ctx, ((0, 0), (0, cols - chans))), col_table)
    got = lax.all_to_all(messages, "rows", split_axis=0, concat_axis=0, tiled=True)

    count = blocks * columns
    joined = pl.pallas_call(
        functools.partial(
            main_kernel, (blocks, frames, columns, chans, rows, total, cols, wide)
        ),
        out_shape=jax.ShapeDtypeStruct((rows, wide, cols), BF),
        in_specs=[smem, vmem, vmem, vmem, vmem],
        out_specs=vmem,
        scratch_shapes=[
            pltpu.VMEM((frames * chans, count), BF),
            pltpu.VMEM((span, 32, count), F32),
            pltpu.VMEM((3 * rows, cols), F32),
            pltpu.VMEM((span, frames * chans, cols), BF),
            pltpu.VMEM((rows + 4, frames * chans, cols), BF),
            pltpu.VMEM((rows + 2, wide, cols), BF),
        ],
        compiler_params=pltpu.CompilerParams(vmem_limit_bytes=56 * 1024 * 1024),
        name="main",
    )(scal, got, taps(w_bev), taps(w_join), taps(w_out))
    return joined[None]


def solution(mesh):
    in_specs = (
        P("tm", "rows", None),
        P(),
        P(),
        P("rows", None),
        P(),
        P("tm", None, None),
        P(),
        P(),
    )
    out_specs = P("tm", "rows", None, None)
    return jax.shard_map(shards, mesh=mesh, in_specs=in_specs, out_specs=out_specs, check_vma=False)
```

```python
import functools

import jax
import jax.numpy as jnp
from jax import lax
from jax.experimental import pallas as pl
from jax.experimental.pallas import tpu as pltpu
from jax.sharding import PartitionSpec as P

BF = jnp.bfloat16
F32 = jnp.float32
EXTRA = 7
REACH = 4
GROUP = 3


def silu(v):
    return v / (1.0 + jnp.exp(-v))


def spread(acc, lane, chans):
    cols = acc.shape[1]
    low = jnp.where(lane == 0, 0.0, pltpu.roll(acc[:chans], 1, 1))
    high = jnp.where(lane == cols - 1, 0.0, pltpu.roll(acc[2 * chans :], cols - 1, 1))
    return acc[chans : 2 * chans] + low + high


def pack_kernel(shape, scal, feats, w_depth, w_ctx, table, out, stack):
    blocks, share, columns, chans, rows, total = shape
    span = rows + 2 * EXTRA
    for slot in range(share):
        source = scal[1] + slot
        piece = feats[jnp.maximum(source, 0)]
        stack[slot * columns : (slot + 1) * columns, :] = jnp.where(
            source >= 0, piece, jnp.zeros_like(piece)
        )
    stacked = stack[...]
    depth = jax.nn.sigmoid(jnp.dot(stacked, w_depth[...], preferred_element_type=F32))
    main = depth.astype(BF).astype(F32)
    rest = depth - main
    ctx = jnp.dot(stacked, w_ctx[...], preferred_element_type=F32)
    lane = lax.broadcasted_iota(jnp.int32, ctx.shape, 1)
    tab = jnp.concatenate([table[...].astype(F32), jnp.zeros_like(table[...]).astype(F32)], axis=0)
    cols = depth.shape[1]
    for block in range(blocks):
        first = rows * block - EXTRA
        message = jnp.where(lane < chans, ctx, 0.0)
        for part, values in enumerate((main, rest)):
            start = chans + part * span
            turned = pltpu.roll(values, (start - first) % cols, 1)
            low = max(start, start - first)
            high = min(start + span, total - first + start)
            message = jnp.where((lane >= low) & (lane < high), turned, message)
        out[block, : share * columns, :] = message.astype(BF)
        out[block, share * columns :, :] = tab.astype(BF)


def lift_and_convolve(shape, scal, got, tabled, w_bev, store, ctx, dep, tab, lifted, skip, last, frames):
    blocks, share, columns, chans, rows, total, cols, wide = shape
    here = scal[0]
    count = blocks * columns
    span = rows + 2 * EXTRA

    for i in range(frames):
        at = (skip + i) * columns
        if not isinstance(at, int):
            at = pl.multiple_of(at, 16)
        piece = got[:, pl.ds(at, columns), :].reshape(count, cols)
        turned = piece.astype(F32).T
        ctx[i * chans : (i + 1) * chans, :] = turned[:chans].astype(BF)
        dep[:, i, :] = turned[chans : chans + span]
        dep[:, 16 + i, :] = turned[chans + span : chans + 2 * span]
    for side in range(3):
        block = jnp.clip(here + (side - 1), 0, blocks - 1)
        both = tabled[block, share * columns :, :].astype(F32)
        tab[side * rows : (side + 1) * rows, :] = both[:rows]

    number = lax.broadcasted_iota(jnp.int32, (count, cols), 0)

    def lift(pair, carry):
        hots = []
        gains = []
        for half in range(2):
            row = 2 * pair + half
            seen = tab[pl.ds(row + rows - EXTRA, 1), :].astype(jnp.int32)
            hot = jnp.where(number == seen, 1.0, 0.0).astype(BF)
            hots.append(hot)
            both = jnp.dot(dep[row].astype(BF), hot, preferred_element_type=F32)
            gains.append(both[:16] + both[16:])
        hot = jnp.concatenate(hots, axis=1)
        for start in range(0, frames, GROUP):
            stop = min(start + GROUP, frames)
            picked = jnp.dot(
                ctx[start * chans : stop * chans, :], hot, preferred_element_type=F32
            )
            for i in range(start, stop):
                part = picked[(i - start) * chans : (i - start + 1) * chans]
                for half in range(2):
                    value = part[:, half * cols : (half + 1) * cols] * gains[half][i : i + 1, :]
                    lifted[2 * pair + half, i * chans : (i + 1) * chans, :] = value.astype(BF)
        return carry

    lax.fori_loop(0, span // 2, lift, 0)

    lane = lax.broadcasted_iota(jnp.int32, (chans, cols), 1)
    need = rows + 4

    def bev(i, carry):
        k = last - i
        dy = scal[4 + 2 * k]
        dx = scal[5 + 2 * k]
        base = dy + REACH
        at = pl.multiple_of(i * chans, 16)
        inside = (lane + dx >= 0) & (lane + dx < cols)
        turn = jnp.where(dx > 0, cols - dx, -dx)
        for pair in range(need // 2):
            sides = [
                lifted[pl.ds(base + 2 * pair + half, 3), pl.ds(at, chans), :].reshape(3 * chans, cols)
                for half in range(2)
            ]
            acc = jnp.dot(w_bev[...], jnp.concatenate(sides, axis=1), preferred_element_type=F32)
            for half in range(2):
                row = here * rows - 2 + dy + 2 * pair + half
                value = silu(spread(acc[:, half * cols : (half + 1) * cols], lane, chans))
                value = pltpu.roll(value, turn, 1)
                keep = inside & (row >= 0) & (row < total)
                store(2 * pair + half, i, jnp.where(keep, value, 0.0).astype(BF))
        return carry

    lax.fori_loop(0, frames, bev, 0)


def own_kernel(shape, scal, got, w_bev, out, ctx, dep, tab, lifted):
    blocks, share, columns, chans, rows, total, cols, wide = shape

    def store(j, i, value):
        at = pl.multiple_of((share - 1 - i) * chans, 16)
        out[j, pl.ds(at, chans), :] = value

    lift_and_convolve(
        shape, scal, got, got, w_bev, store, ctx, dep, tab, lifted, 0, scal[2], share
    )


def join_kernel(
    shape, scal, got, other, own, w_bev, w_join, w_out, out, ctx, dep, tab, lifted, moved, hidden
):
    blocks, share, columns, chans, rows, total, cols, wide = shape
    here = scal[0]
    rest = share - 1
    last = scal[3]

    def store(j, i, value):
        at = pl.multiple_of((last - i) * chans, 16)
        moved[j, pl.ds(at, chans), :] = value

    lift_and_convolve(
        shape, scal, other, got, w_bev, store, ctx, dep, tab, lifted, jnp.where(last > rest, 1, 0), last, rest
    )
    at = pl.multiple_of((scal[2] - rest) * chans, 16)
    for j in range(rows + 4):
        moved[j, pl.ds(at, share * chans), :] = own[j]

    lane_wide = lax.broadcasted_iota(jnp.int32, (wide, cols), 1)

    def join(pair, carry):
        acc = None
        for a in range(3):
            both = jnp.concatenate([moved[2 * pair + a], moved[2 * pair + 1 + a]], axis=1)
            part = jnp.dot(w_join[a], both, preferred_element_type=F32)
            acc = part if acc is None else acc + part
        for half in range(2):
            row = here * rows - 1 + 2 * pair + half
            value = silu(spread(acc[:, half * cols : (half + 1) * cols], lane_wide, wide))
            keep = (row >= 0) & (row < total)
            hidden[2 * pair + half] = jnp.where(keep, value, 0.0).astype(BF)
        return carry

    lax.fori_loop(0, (rows + 2) // 2, join, 0)

    def close(pair, carry):
        sides = [hidden[pl.ds(2 * pair + half, 3), :, :].reshape(3 * wide, cols) for half in range(2)]
        acc = jnp.dot(w_out[...], jnp.concatenate(sides, axis=1), preferred_element_type=F32)
        for half in range(2):
            value = spread(acc[:, half * cols : (half + 1) * cols], lane_wide, wide)
            out[2 * pair + half] = value.astype(BF)
        return carry

    lax.fori_loop(0, rows // 2, close, 0)


def taps(weight):
    turned = jnp.transpose(weight, (1, 3, 0, 2))
    return turned.reshape(weight.shape[1] * weight.shape[3], weight.shape[0] * weight.shape[2])


VMEM = pl.BlockSpec(memory_space=pltpu.VMEM)
SMEM = pl.BlockSpec(memory_space=pltpu.SMEM)


def scratch(frames, chans, count, rows, cols):
    span = rows + 2 * EXTRA
    return [
        pltpu.VMEM((frames * chans, count), BF),
        pltpu.VMEM((span, 32, count), F32),
        pltpu.VMEM((3 * rows, cols), F32),
        pltpu.VMEM((span, frames * chans, cols), BF),
    ]


def call_pack(shape, scal, feats, w_depth, w_ctx, table):
    blocks, share, columns, chans, rows, total, cols, wide = shape
    return pl.pallas_call(
        functools.partial(pack_kernel, shape[:6]),
        out_shape=jax.ShapeDtypeStruct((blocks, share * columns + 2 * rows, cols), BF),
        in_specs=[SMEM, VMEM, VMEM, VMEM, VMEM],
        out_specs=VMEM,
        scratch_shapes=[pltpu.VMEM((share * columns, feats.shape[2]), BF)],
        compiler_params=pltpu.CompilerParams(vmem_limit_bytes=32 * 1024 * 1024),
        name="pack",
    )(scal, feats, w_depth, w_ctx, table)


def call_own(shape, scal, got, w_bev):
    blocks, share, columns, chans, rows, total, cols, wide = shape
    return pl.pallas_call(
        functools.partial(own_kernel, shape),
        out_shape=jax.ShapeDtypeStruct((rows + 4, share * chans, cols), BF),
        in_specs=[SMEM, VMEM, VMEM],
        out_specs=VMEM,
        scratch_shapes=scratch(share, chans, blocks * columns, rows, cols),
        compiler_params=pltpu.CompilerParams(vmem_limit_bytes=32 * 1024 * 1024),
        name="own",
    )(scal, got, w_bev)


def call_join(shape, scal, got, other, own, w_bev, w_join, w_out):
    blocks, share, columns, chans, rows, total, cols, wide = shape
    return pl.pallas_call(
        functools.partial(join_kernel, shape),
        out_shape=jax.ShapeDtypeStruct((rows, wide, cols), BF),
        in_specs=[SMEM] + [VMEM] * 6,
        out_specs=VMEM,
        scratch_shapes=scratch(share - 1, chans, blocks * columns, rows, cols)
        + [
            pltpu.VMEM((rows + 4, (2 * share - 1) * chans, cols), BF),
            pltpu.VMEM((rows + 2, wide, cols), BF),
        ],
        compiler_params=pltpu.CompilerParams(vmem_limit_bytes=48 * 1024 * 1024),
        name="join",
    )(scal, got, other, own, w_bev, w_join, w_out)


def shards(col_feat, w_depth, w_ctx, col_table, w_bev, offsets, w_join, w_out):
    rows, cols = col_table.shape
    frames = offsets.shape[1] + 1
    chans = w_ctx.shape[1]
    wide = w_out.shape[3]
    columns, depth_k = col_feat.shape[1:]
    blocks = lax.axis_size("rows")
    window = lax.axis_size("tm")
    total = w_depth.shape[1]
    share = (frames + 1) // 2
    shape = (blocks, share, columns, chans, rows, total, cols, wide)

    feats = jnp.broadcast_to(col_feat, (window, columns, depth_k))
    feats = lax.all_to_all(feats, "tm", split_axis=0, concat_axis=0, tiled=True)
    w_ctx = jnp.pad(w_ctx, ((0, 0), (0, cols - chans)))
    feats, w_ctx, w_bev, w_out = lax.optimization_barrier((feats, w_ctx, taps(w_bev), taps(w_out)))

    frame = lax.axis_index("tm").astype(jnp.int32)
    core = frame % 2
    head = jnp.stack(
        [
            lax.axis_index("rows").astype(jnp.int32),
            frame - core - (frames - 1) + share * core,
            frames - 1 - (share - 1) * core,
            share - 2 + share * core,
        ]
    )
    moves = jnp.concatenate([jnp.zeros((1, 2), jnp.int32), offsets[0]], axis=0)
    scal = jnp.concatenate([head, moves.reshape(-1)])

    messages = call_pack(shape, scal, feats, w_depth, w_ctx, col_table)
    got = lax.all_to_all(messages, "rows", split_axis=0, concat_axis=0, tiled=True)
    other = lax.ppermute(got, "tm", [(i, i ^ 1) for i in range(window)])

    w_join = jnp.transpose(w_join, (0, 1, 3, 2)).reshape(3, 3 * wide, frames * chans)
    own = call_own(shape, scal, got, w_bev)
    joined = call_join(shape, scal, got, other, own, w_bev, w_join, w_out)
    return joined[None]


def solution(mesh):
    in_specs = (
        P("tm", "rows", None),
        P(),
        P(),
        P("rows", None),
        P(),
        P("tm", None, None),
        P(),
        P(),
    )
    out_specs = P("tm", "rows", None, None)
    return jax.shard_map(shards, mesh=mesh, in_specs=in_specs, out_specs=out_specs, check_vma=False)
```

```python
import functools

import jax
import jax.numpy as jnp
from jax import lax
from jax.experimental import pallas as pl
from jax.experimental.pallas import tpu as pltpu
from jax.sharding import PartitionSpec as P

BF = jnp.bfloat16
F32 = jnp.float32
EXTRA = 7
REACH = 4
GROUP = 3
LIFT = 22
BEV = 2
JOIN = 10
CLOSE = 8


def silu(v):
    return v / (1.0 + jnp.exp(-v))


def spread(acc, lane, chans):
    cols = acc.shape[1]
    low = jnp.where(lane == 0, 0.0, pltpu.roll(acc[:chans], 1, 1))
    high = jnp.where(lane == cols - 1, 0.0, pltpu.roll(acc[2 * chans :], cols - 1, 1))
    return acc[chans : 2 * chans] + low + high


def pack_kernel(shape, scal, feats, w_depth, w_ctx, out, stack):
    blocks, share, columns, chans, rows, total = shape
    span = rows + 2 * EXTRA
    for slot in range(share):
        source = scal[1] + slot
        piece = feats[jnp.maximum(source, 0)]
        stack[slot * columns : (slot + 1) * columns, :] = jnp.where(
            source >= 0, piece, jnp.zeros_like(piece)
        )
    stacked = stack[...]
    depth = jax.nn.sigmoid(jnp.dot(stacked, w_depth[...], preferred_element_type=F32))
    main = depth.astype(BF).astype(F32)
    rest = depth - main
    ctx = jnp.dot(stacked, w_ctx[...], preferred_element_type=F32)
    lane = lax.broadcasted_iota(jnp.int32, ctx.shape, 1)
    cols = depth.shape[1]
    for block in range(blocks):
        first = rows * block - EXTRA
        message = jnp.where(lane < chans, ctx, 0.0)
        for part, values in enumerate((main, rest)):
            start = chans + part * span
            turned = pltpu.roll(values, (start - first) % cols, 1)
            low = max(start, start - first)
            high = min(start + span, total - first + start)
            message = jnp.where((lane >= low) & (lane < high), turned, message)
        out[block] = message.astype(BF)


def lift_and_convolve(shape, scal, got, tables, w_bev, store, ctx, dep, tab, lifted, skip, last, frames):
    blocks, share, columns, chans, rows, total, cols, wide = shape
    here = scal[0]
    count = blocks * columns
    span = rows + 2 * EXTRA

    for i in range(frames):
        at = (skip + i) * columns
        if not isinstance(at, int):
            at = pl.multiple_of(at, 16)
        piece = got[:, pl.ds(at, columns), :].reshape(count, cols)
        turned = piece.astype(F32).T
        ctx[i * chans : (i + 1) * chans, :] = turned[:chans].astype(BF)
        dep[:, i, :] = turned[chans : chans + span]
        dep[:, 16 + i, :] = turned[chans + span : chans + 2 * span]
    for side in range(3):
        tab[side * rows : (side + 1) * rows, :] = tables[side][...]

    number = lax.broadcasted_iota(jnp.int32, (count, cols), 0)

    def lift(pair, carry):
        hots = []
        gains = []
        for half in range(LIFT):
            row = LIFT * pair + half
            seen = tab[pl.ds(row + rows - EXTRA, 1), :]
            hot = jnp.where(number == seen, 1.0, 0.0).astype(BF)
            hots.append(hot)
            both = jnp.dot(dep[row].astype(BF), hot, preferred_element_type=F32)
            gains.append(both[:16] + both[16:])
        hot = jnp.concatenate(hots, axis=1)
        for start in range(0, frames, GROUP):
            stop = min(start + GROUP, frames)
            picked = jnp.dot(
                ctx[start * chans : stop * chans, :], hot, preferred_element_type=F32
            )
            for i in range(start, stop):
                part = picked[(i - start) * chans : (i - start + 1) * chans]
                for half in range(LIFT):
                    value = part[:, half * cols : (half + 1) * cols] * gains[half][i : i + 1, :]
                    lifted[LIFT * pair + half, i * chans : (i + 1) * chans, :] = value.astype(BF)
        return carry

    lax.fori_loop(0, span // LIFT, lift, 0)

    lane = lax.broadcasted_iota(jnp.int32, (chans, cols), 1)
    need = rows + 4

    def bev(i, carry):
        k = last - 2 * i
        dy = scal[3 + 2 * k]
        dx = scal[4 + 2 * k]
        base = dy + REACH
        at = pl.multiple_of(i * chans, 16)
        inside = (lane + dx >= 0) & (lane + dx < cols)
        turn = jnp.where(dx > 0, cols - dx, -dx)
        for pair in range(need // BEV):
            sides = [
                lifted[pl.ds(base + BEV * pair + half, 3), pl.ds(at, chans), :].reshape(3 * chans, cols)
                for half in range(BEV)
            ]
            acc = jnp.dot(w_bev[...], jnp.concatenate(sides, axis=1), preferred_element_type=F32)
            for half in range(BEV):
                row = here * rows - 2 + dy + BEV * pair + half
                value = silu(spread(acc[:, half * cols : (half + 1) * cols], lane, chans))
                value = pltpu.roll(value, turn, 1)
                keep = inside & (row >= 0) & (row < total)
                store(BEV * pair + half, i, jnp.where(keep, value, 0.0).astype(BF))
        return carry

    lax.fori_loop(0, frames, bev, 0)


def own_kernel(shape, scal, got, low, mid, high, w_bev, out, ctx, dep, tab, lifted):
    share, chans = shape[1], shape[3]

    def store(j, i, value):
        out[j, pl.ds(pl.multiple_of(i * chans, 16), chans), :] = value

    lift_and_convolve(
        shape, scal, got, (low, mid, high), w_bev, store, ctx, dep, tab, lifted, 0, 2 * share - 2, share
    )


def join_kernel(
    shape, scal, other, low, mid, high, own, w_bev, w_join, w_out, out, ctx, dep, tab, lifted, moved, hidden
):
    blocks, share, columns, chans, rows, total, cols, wide = shape
    here = scal[0]
    last = 2 * share - 3

    def store(j, i, value):
        moved[j, pl.ds(pl.multiple_of((last - 2 * i) * chans, 16), chans), :] = value

    lift_and_convolve(
        shape, scal, other, (low, mid, high), w_bev, store, ctx, dep, tab, lifted, scal[2], last, share - 1
    )
    for i in range(share):
        at = (2 * share - 2 - 2 * i) * chans
        for j in range(rows + 4):
            moved[j, at : at + chans, :] = own[j, i * chans : (i + 1) * chans, :]

    lane_wide = lax.broadcasted_iota(jnp.int32, (wide, cols), 1)

    def join(pair, carry):
        acc = None
        for a in range(3):
            both = jnp.concatenate([moved[JOIN * pair + h + a] for h in range(JOIN)], axis=1)
            part = jnp.dot(w_join[a], both, preferred_element_type=F32)
            acc = part if acc is None else acc + part
        for half in range(JOIN):
            row = here * rows - 1 + JOIN * pair + half
            value = silu(spread(acc[:, half * cols : (half + 1) * cols], lane_wide, wide))
            keep = (row >= 0) & (row < total)
            hidden[JOIN * pair + half] = jnp.where(keep, value, 0.0).astype(BF)
        return carry

    lax.fori_loop(0, (rows + 2) // JOIN, join, 0)

    def close(pair, carry):
        sides = [hidden[pl.ds(CLOSE * pair + half, 3), :, :].reshape(3 * wide, cols) for half in range(CLOSE)]
        acc = jnp.dot(w_out[...], jnp.concatenate(sides, axis=1), preferred_element_type=F32)
        for half in range(CLOSE):
            value = spread(acc[:, half * cols : (half + 1) * cols], lane_wide, wide)
            out[CLOSE * pair + half] = value.astype(BF)
        return carry

    lax.fori_loop(0, rows // CLOSE, close, 0)


def taps(weight):
    turned = jnp.transpose(weight, (1, 3, 0, 2))
    return turned.reshape(weight.shape[1] * weight.shape[3], weight.shape[0] * weight.shape[2])


VMEM = pl.BlockSpec(memory_space=pltpu.VMEM)
SMEM = pl.BlockSpec(memory_space=pltpu.SMEM)


def scratch(frames, chans, count, rows, cols):
    span = rows + 2 * EXTRA
    return [
        pltpu.VMEM((frames * chans, count), BF),
        pltpu.VMEM((span, 32, count), F32),
        pltpu.VMEM((3 * rows, cols), jnp.int32),
        pltpu.VMEM((span, frames * chans, cols), BF),
    ]


def call_pack(shape, scal, feats, w_depth, w_ctx):
    blocks, share, columns, chans, rows, total, cols, wide = shape
    return pl.pallas_call(
        functools.partial(pack_kernel, shape[:6]),
        out_shape=jax.ShapeDtypeStruct((blocks, share * columns, cols), BF),
        in_specs=[SMEM, VMEM, VMEM, VMEM],
        out_specs=VMEM,
        scratch_shapes=[pltpu.VMEM((share * columns, feats.shape[2]), BF)],
        compiler_params=pltpu.CompilerParams(vmem_limit_bytes=32 * 1024 * 1024),
        name="pack",
    )(scal, feats, w_depth, w_ctx)


def call_own(shape, scal, got, tables, w_bev):
    blocks, share, columns, chans, rows, total, cols, wide = shape
    return pl.pallas_call(
        functools.partial(own_kernel, shape),
        out_shape=jax.ShapeDtypeStruct((rows + 4, share * chans, cols), BF),
        in_specs=[SMEM] + [VMEM] * 5,
        out_specs=VMEM,
        scratch_shapes=scratch(share, chans, blocks * columns, rows, cols),
        compiler_params=pltpu.CompilerParams(vmem_limit_bytes=24 * 1024 * 1024),
        name="own",
    )(scal, got, *tables, w_bev)


def call_join(shape, scal, other, tables, own, w_bev, w_join, w_out):
    blocks, share, columns, chans, rows, total, cols, wide = shape
    return pl.pallas_call(
        functools.partial(join_kernel, shape),
        out_shape=jax.ShapeDtypeStruct((rows, wide, cols), BF),
        in_specs=[SMEM] + [VMEM] * 8,
        out_specs=VMEM,
        scratch_shapes=scratch(share - 1, chans, blocks * columns, rows, cols)
        + [
            pltpu.VMEM((rows + 4, (2 * share - 1) * chans, cols), BF),
            pltpu.VMEM((rows + 2, wide, cols), BF),
        ],
        compiler_params=pltpu.CompilerParams(vmem_limit_bytes=36 * 1024 * 1024),
        name="join",
    )(scal, other, *tables, own, w_bev, w_join, w_out)


def shards(col_feat, w_depth, w_ctx, col_table, w_bev, offsets, w_join, w_out):
    rows, cols = col_table.shape
    frames = offsets.shape[1] + 1
    chans = w_ctx.shape[1]
    wide = w_out.shape[3]
    columns, depth_k = col_feat.shape[1:]
    blocks = lax.axis_size("rows")
    window = lax.axis_size("tm")
    total = w_depth.shape[1]
    share = (frames + 1) // 2
    shape = (blocks, share, columns, chans, rows, total, cols, wide)

    feats = jnp.broadcast_to(col_feat, (window // 2, columns, depth_k))
    groups = [list(range(core, window, 2)) for core in range(2)]
    feats = lax.all_to_all(
        feats, "tm", split_axis=0, concat_axis=0, axis_index_groups=groups, tiled=True
    )
    up = [(i, i + 1) for i in range(blocks - 1)]
    tables = (
        lax.ppermute(col_table, "rows", up),
        col_table,
        lax.ppermute(col_table, "rows", [(t, s) for s, t in up]),
    )
    w_ctx = jnp.pad(w_ctx, ((0, 0), (0, cols - chans)))
    feats, tables, w_ctx, w_bev, w_out = lax.optimization_barrier(
        (feats, tables, w_ctx, taps(w_bev), taps(w_out))
    )

    frame = lax.axis_index("tm").astype(jnp.int32)
    head = jnp.stack(
        [lax.axis_index("rows").astype(jnp.int32), (frame >> 1) - (share - 1), frame & 1]
    )
    moves = jnp.concatenate([jnp.zeros((1, 2), jnp.int32), offsets[0]], axis=0)
    scal = jnp.concatenate([head, moves.reshape(-1)])

    messages = call_pack(shape, scal, feats, w_depth, w_ctx)
    got = lax.all_to_all(messages, "rows", split_axis=0, concat_axis=0, tiled=True)
    other = lax.ppermute(got, "tm", [(i, i ^ 1) for i in range(window)])

    w_join = jnp.transpose(w_join, (0, 1, 3, 2)).reshape(3, 3 * wide, frames * chans)
    own = call_own(shape, scal, got, tables, w_bev)
    joined = call_join(shape, scal, other, tables, own, w_bev, w_join, w_out)
    return joined[None]


def solution(mesh):
    in_specs = (
        P("tm", "rows", None),
        P(),
        P(),
        P("rows", None),
        P(),
        P("tm", None, None),
        P(),
        P(),
    )
    out_specs = P("tm", "rows", None, None)
    return jax.shard_map(shards, mesh=mesh, in_specs=in_specs, out_specs=out_specs, check_vma=False)
```

```python
import functools

import jax
import jax.numpy as jnp
from jax import lax
from jax.experimental import pallas as pl
from jax.experimental.pallas import tpu as pltpu
from jax.sharding import Mesh
from jax.sharding import PartitionSpec as P

BF = jnp.bfloat16
F32 = jnp.float32
EXTRA = 7
REACH = 4
GROUP = 3
LIFT = 22
BEV = 2
JOIN = 10
CLOSE = 8


def silu(v):
    return v / (1.0 + jnp.exp(-v))


def spread(acc, lane, chans):
    cols = acc.shape[1]
    low = jnp.where(lane == 0, 0.0, pltpu.roll(acc[:chans], 1, 1))
    high = jnp.where(lane == cols - 1, 0.0, pltpu.roll(acc[2 * chans :], cols - 1, 1))
    return acc[chans : 2 * chans] + low + high


def pack_kernel(shape, scal, feats, w_depth, w_ctx, out, stack):
    ranks, share, columns, chans, rows, total, cols, wide = shape
    span = rows + 2 * EXTRA
    far = scal[3]
    alone = feats.shape[1]
    for slot in range(share):
        source = scal[1] + slot
        for part in range(columns // alone):
            piece = feats[jnp.maximum(source, 0) * (columns // alone) + part]
            at = slot * columns + part * alone
            stack[at : at + alone, :] = jnp.where(source >= 0, piece, jnp.zeros_like(piece))
    stacked = stack[...]
    depth = jax.nn.sigmoid(jnp.dot(stacked, w_depth[...], preferred_element_type=F32))
    main = depth.astype(BF).astype(F32)
    rest = depth - main
    ctx = jnp.dot(stacked, w_ctx[...], preferred_element_type=F32)
    lane = lax.broadcasted_iota(jnp.int32, ctx.shape, 1)
    for rank in range(ranks):
        first = rows * (rank // 2 * 4 + rank % 2 + 2 * far) - EXTRA
        message = jnp.where(lane < chans, ctx, 0.0)
        for part, values in enumerate((main, rest)):
            start = chans + part * span
            turned = pltpu.roll(values, lax.rem(start - first + total, total), 1)
            low = jnp.maximum(start, start - first)
            high = jnp.minimum(start + span, total - first + start)
            message = jnp.where((lane >= low) & (lane < high), turned, message)
        out[rank] = message.astype(BF)


def lift_and_convolve(shape, scal, got, tables, w_bev, store, ctx, dep, tab, lifted, skip, last, frames):
    ranks, share, columns, chans, rows, total, cols, wide = shape
    here = scal[0]
    count = ranks * columns
    span = rows + 2 * EXTRA

    for i in range(frames):
        at = (skip + i) * columns
        if not isinstance(at, int):
            at = pl.multiple_of(at, 16)
        piece = got[:, pl.ds(at, columns), :].reshape(count, cols)
        turned = piece.T.astype(F32)
        ctx[i * chans : (i + 1) * chans, :] = turned[:chans].astype(BF)
        dep[:, i, :] = turned[chans : chans + span]
        dep[:, 16 + i, :] = turned[chans + span : chans + 2 * span]
    for side in range(3):
        tab[side * rows : (side + 1) * rows, :] = tables[side][...]

    alone = columns // 2
    place = lax.broadcasted_iota(jnp.int32, (count, cols), 0)
    number = (place & ~(3 * alone)) | ((place & alone) << 1) | ((place & (2 * alone)) >> 1)

    def lift(pair, carry):
        hots = []
        gains = []
        for half in range(LIFT):
            row = LIFT * pair + half
            seen = tab[pl.ds(row + rows - EXTRA, 1), :]
            hot = jnp.where(number == seen, 1.0, 0.0).astype(BF)
            hots.append(hot)
            both = jnp.dot(dep[row].astype(BF), hot, preferred_element_type=F32)
            gains.append(both[:16] + both[16:])
        hot = jnp.concatenate(hots, axis=1)
        for start in range(0, frames, GROUP):
            stop = min(start + GROUP, frames)
            picked = jnp.dot(
                ctx[start * chans : stop * chans, :], hot, preferred_element_type=F32
            )
            for i in range(start, stop):
                part = picked[(i - start) * chans : (i - start + 1) * chans]
                for half in range(LIFT):
                    value = part[:, half * cols : (half + 1) * cols] * gains[half][i : i + 1, :]
                    lifted[LIFT * pair + half, i * chans : (i + 1) * chans, :] = value.astype(BF)
        return carry

    lax.fori_loop(0, span // LIFT, lift, 0)

    lane = lax.broadcasted_iota(jnp.int32, (chans, cols), 1)
    need = rows + 4

    def bev(i):
        k = last - 2 * i
        dy = scal[4 + 2 * k]
        dx = scal[5 + 2 * k]
        base = dy + REACH
        at = i * chans
        inside = (lane + dx >= 0) & (lane + dx < cols)
        turn = jnp.where(dx > 0, cols - dx, -dx)
        for pair in range(need // BEV):
            sides = [
                lifted[pl.ds(base + BEV * pair + half, 3), at : at + chans, :].reshape(3 * chans, cols)
                for half in range(BEV)
            ]
            acc = jnp.dot(w_bev[...], jnp.concatenate(sides, axis=1), preferred_element_type=F32)
            for half in range(BEV):
                row = here * rows - 2 + dy + BEV * pair + half
                value = silu(spread(acc[:, half * cols : (half + 1) * cols], lane, chans))
                value = pltpu.roll(value, turn, 1)
                keep = inside & (row >= 0) & (row < total)
                store(BEV * pair + half, i, jnp.where(keep, value, 0.0).astype(BF))

    for i in range(frames):
        bev(i)


def own_kernel(shape, scal, got, low, mid, high, w_bev, out, ctx, dep, tab, lifted):
    share, chans = shape[1], shape[3]

    def store(j, i, value):
        out[j, i * chans : (i + 1) * chans, :] = value

    lift_and_convolve(
        shape, scal, got, (low, mid, high), w_bev, store, ctx, dep, tab, lifted, 0, 2 * share - 2, share
    )


def join_kernel(
    shape, scal, other, low, mid, high, own, w_bev, w_join, w_out, out, ctx, dep, tab, lifted, moved, hidden
):
    ranks, share, columns, chans, rows, total, cols, wide = shape
    here = scal[0]
    last = 2 * share - 3

    def store(j, i, value):
        moved[j, (last - 2 * i) * chans : (last - 2 * i + 1) * chans, :] = value

    lift_and_convolve(
        shape, scal, other, (low, mid, high), w_bev, store, ctx, dep, tab, lifted, scal[2], last, share - 1
    )
    for i in range(share):
        at = (2 * share - 2 - 2 * i) * chans
        for j in range(rows + 4):
            moved[j, at : at + chans, :] = own[j, i * chans : (i + 1) * chans, :]

    lane_wide = lax.broadcasted_iota(jnp.int32, (wide, cols), 1)

    def join(pair, carry):
        acc = None
        for a in range(3):
            both = jnp.concatenate([moved[JOIN * pair + h + a] for h in range(JOIN)], axis=1)
            part = jnp.dot(w_join[a], both, preferred_element_type=F32)
            acc = part if acc is None else acc + part
        for half in range(JOIN):
            row = here * rows - 1 + JOIN * pair + half
            value = silu(spread(acc[:, half * cols : (half + 1) * cols], lane_wide, wide))
            keep = (row >= 0) & (row < total)
            hidden[JOIN * pair + half] = jnp.where(keep, value, 0.0).astype(BF)
        return carry

    lax.fori_loop(0, (rows + 2) // JOIN, join, 0)

    def close(pair, carry):
        sides = [hidden[pl.ds(CLOSE * pair + half, 3), :, :].reshape(3 * wide, cols) for half in range(CLOSE)]
        acc = jnp.dot(w_out[...], jnp.concatenate(sides, axis=1), preferred_element_type=F32)
        for half in range(CLOSE):
            value = spread(acc[:, half * cols : (half + 1) * cols], lane_wide, wide)
            out[CLOSE * pair + half] = value.astype(BF)
        return carry

    lax.fori_loop(0, rows // CLOSE, close, 0)


def taps(weight):
    turned = jnp.transpose(weight, (1, 3, 0, 2))
    return turned.reshape(weight.shape[1] * weight.shape[3], weight.shape[0] * weight.shape[2])


VMEM = pl.BlockSpec(memory_space=pltpu.VMEM)
SMEM = pl.BlockSpec(memory_space=pltpu.SMEM)


def scratch(frames, chans, count, rows, cols):
    span = rows + 2 * EXTRA
    return [
        pltpu.VMEM((frames * chans, count), BF),
        pltpu.VMEM((span, 32, count), F32),
        pltpu.VMEM((3 * rows, cols), jnp.int32),
        pltpu.VMEM((span, frames * chans, cols), BF),
    ]


def call_pack(shape, scal, feats, w_depth, w_ctx):
    ranks, share, columns, chans, rows, total, cols, wide = shape
    return pl.pallas_call(
        functools.partial(pack_kernel, shape),
        out_shape=jax.ShapeDtypeStruct((ranks, share * columns, cols), BF),
        in_specs=[SMEM, VMEM, VMEM, VMEM],
        out_specs=VMEM,
        scratch_shapes=[pltpu.VMEM((share * columns, feats.shape[2]), BF)],
        compiler_params=pltpu.CompilerParams(vmem_limit_bytes=32 * 1024 * 1024),
        name="pack",
    )(scal, feats, w_depth, w_ctx)


def call_own(shape, scal, got, tables, w_bev):
    ranks, share, columns, chans, rows, total, cols, wide = shape
    return pl.pallas_call(
        functools.partial(own_kernel, shape),
        out_shape=jax.ShapeDtypeStruct((rows + 4, share * chans, cols), BF),
        in_specs=[SMEM] + [VMEM] * 5,
        out_specs=VMEM,
        scratch_shapes=scratch(share, chans, ranks * columns, rows, cols),
        compiler_params=pltpu.CompilerParams(vmem_limit_bytes=24 * 1024 * 1024),
        name="own",
    )(scal, got, *tables, w_bev)


def call_join(shape, scal, other, tables, own, w_bev, w_join, w_out):
    ranks, share, columns, chans, rows, total, cols, wide = shape
    return pl.pallas_call(
        functools.partial(join_kernel, shape),
        out_shape=jax.ShapeDtypeStruct((rows, wide, cols), BF),
        in_specs=[SMEM] + [VMEM] * 8,
        out_specs=VMEM,
        scratch_shapes=scratch(share - 1, chans, ranks * columns, rows, cols)
        + [
            pltpu.VMEM((rows + 4, (2 * share - 1) * chans, cols), BF),
            pltpu.VMEM((rows + 2, wide, cols), BF),
        ],
        compiler_params=pltpu.CompilerParams(vmem_limit_bytes=36 * 1024 * 1024),
        name="join",
    )(scal, other, *tables, own, w_bev, w_join, w_out)


def shards(col_feat, w_depth, w_ctx, col_table, w_bev, offsets, w_join, w_out):
    rows, cols = col_table.shape
    frames = offsets.shape[1] + 1
    chans = w_ctx.shape[1]
    wide = w_out.shape[3]
    alone, depth_k = col_feat.shape[1:]
    ranks = lax.axis_size("x") * lax.axis_size("near")
    chips = lax.axis_size("chip")
    total = w_depth.shape[1]
    share = (frames + 1) // 2
    columns = 2 * alone
    shape = (ranks, share, columns, chans, rows, total, cols, wide)
    line = ("x", "far", "near")

    feats = jnp.broadcast_to(col_feat, (chips * 2, alone, depth_k))
    feats = lax.all_to_all(feats, ("chip", "far"), split_axis=0, concat_axis=0, tiled=True)
    up = [(i, i + 1) for i in range(2 * ranks - 1)]
    tables = (
        lax.ppermute(col_table, line, up),
        col_table,
        lax.ppermute(col_table, line, [(t, s) for s, t in up]),
    )
    w_ctx = jnp.pad(w_ctx, ((0, 0), (0, cols - chans)))
    feats, tables, w_ctx, w_bev, w_out = lax.optimization_barrier(
        (feats, tables, w_ctx, taps(w_bev), taps(w_out))
    )

    head = jnp.stack(
        [
            lax.axis_index(line).astype(jnp.int32),
            lax.axis_index("chip").astype(jnp.int32) - (share - 1),
            lax.axis_index("core").astype(jnp.int32),
            lax.axis_index("far").astype(jnp.int32),
        ]
    )
    moves = jnp.concatenate([jnp.zeros((1, 2), jnp.int32), offsets[0]], axis=0)
    scal = jnp.concatenate([head, moves.reshape(-1)])

    messages = call_pack(shape, scal, feats, w_depth, w_ctx)
    got = lax.all_to_all(messages, ("x", "near"), split_axis=0, concat_axis=0, tiled=True)
    other = lax.ppermute(got, "core", [(0, 1), (1, 0)])

    w_join = jnp.transpose(w_join, (0, 1, 3, 2)).reshape(3, 3 * wide, frames * chans)
    own = call_own(shape, scal, got, tables, w_bev)
    joined = call_join(shape, scal, other, tables, own, w_bev, w_join, w_out)
    return joined[None]


def solution(mesh):
    split = Mesh(
        mesh.devices.reshape(mesh.shape["tm"] // 2, 2, mesh.shape["rows"] // 4, 2, 2),
        ("chip", "core", "x", "far", "near"),
    )
    tm, rows = ("chip", "core"), ("x", "far", "near")
    in_specs = (
        P(tm, rows, None),
        P(),
        P(),
        P(rows, None),
        P(),
        P(tm, None, None),
        P(),
        P(),
    )
    out_specs = P(tm, rows, None, None)
    return jax.shard_map(shards, mesh=split, in_specs=in_specs, out_specs=out_specs, check_vma=False)
```

```python
import functools

import jax
import jax.numpy as jnp
from jax import lax
from jax.experimental import pallas as pl
from jax.experimental.pallas import tpu as pltpu
from jax.sharding import Mesh
from jax.sharding import PartitionSpec as P

BF = jnp.bfloat16
F32 = jnp.float32
EXTRA = 7
REACH = 4
GROUP = 3
LIFT = 22
BEV = 2
JOIN = 10
CLOSE = 8


def silu(v):
    return (0.5 * v) * (1.0 + jnp.tanh(0.5 * v))


def spread(acc, lane, chans):
    cols = acc.shape[1]
    low = jnp.where(lane == 0, 0.0, pltpu.roll(acc[:chans], 1, 1))
    high = jnp.where(lane == cols - 1, 0.0, pltpu.roll(acc[2 * chans :], cols - 1, 1))
    return acc[chans : 2 * chans] + low + high


def pack_kernel(shape, scal, feats, w_depth, w_ctx, out, stack):
    ranks, share, columns, chans, rows, total, cols, wide = shape
    span = rows + 2 * EXTRA
    far = scal[3]
    alone = feats.shape[1]
    for slot in range(share):
        source = scal[1] + slot
        for part in range(columns // alone):
            piece = feats[jnp.maximum(source, 0) * (columns // alone) + part]
            at = slot * columns + part * alone
            stack[at : at + alone, :] = jnp.where(source >= 0, piece, jnp.zeros_like(piece))
    stacked = stack[...]
    depth = jax.nn.sigmoid(jnp.dot(stacked, w_depth[...], preferred_element_type=F32))
    main = depth.astype(BF).astype(F32)
    rest = depth - main
    ctx = jnp.dot(stacked, w_ctx[...], preferred_element_type=F32)
    lane = lax.broadcasted_iota(jnp.int32, ctx.shape, 1)
    for rank in range(ranks):
        first = rows * (rank // 2 * 4 + rank % 2 + 2 * far) - EXTRA
        message = jnp.where(lane < chans, ctx, 0.0)
        for part, values in enumerate((main, rest)):
            start = chans + part * span
            turned = pltpu.roll(values, lax.rem(start - first + total, total), 1)
            low = jnp.maximum(start, start - first)
            high = jnp.minimum(start + span, total - first + start)
            message = jnp.where((lane >= low) & (lane < high), turned, message)
        out[rank] = message.astype(BF)


def lift_and_convolve(shape, scal, got, tables, w_bev, store, ctx, dep, tab, lifted, skip, last, frames):
    ranks, share, columns, chans, rows, total, cols, wide = shape
    here = scal[0]
    count = ranks * columns
    span = rows + 2 * EXTRA

    for i in range(frames):
        at = (skip + i) * columns
        if not isinstance(at, int):
            at = pl.multiple_of(at, 16)
        piece = got[:, pl.ds(at, columns), :].reshape(count, cols)
        turned = piece.T.astype(F32)
        ctx[i * chans : (i + 1) * chans, :] = turned[:chans].astype(BF)
        dep[:, i, :] = turned[chans : chans + span]
        dep[:, 16 + i, :] = turned[chans + span : chans + 2 * span]
    for side in range(3):
        tab[side * rows : (side + 1) * rows, :] = tables[side][...]

    alone = columns // 2
    place = lax.broadcasted_iota(jnp.int32, (count, cols), 0)
    number = (place & ~(3 * alone)) | ((place & alone) << 1) | ((place & (2 * alone)) >> 1)

    def lift(pair, carry):
        hots = []
        gains = []
        for half in range(LIFT):
            row = LIFT * pair + half
            seen = tab[pl.ds(row + rows - EXTRA, 1), :]
            hot = jnp.where(number == seen, 1.0, 0.0).astype(BF)
            hots.append(hot)
            both = jnp.dot(dep[row].astype(BF), hot, preferred_element_type=F32)
            gains.append(both[:16] + both[16:])
        hot = jnp.concatenate(hots, axis=1)
        for start in range(0, frames, GROUP):
            stop = min(start + GROUP, frames)
            picked = jnp.dot(
                ctx[start * chans : stop * chans, :], hot, preferred_element_type=F32
            )
            for i in range(start, stop):
                part = picked[(i - start) * chans : (i - start + 1) * chans]
                for half in range(LIFT):
                    value = part[:, half * cols : (half + 1) * cols] * gains[half][i : i + 1, :]
                    lifted[LIFT * pair + half, i * chans : (i + 1) * chans, :] = value.astype(BF)
        return carry

    lax.fori_loop(0, span // LIFT, lift, 0)

    lane = lax.broadcasted_iota(jnp.int32, (chans, cols), 1)
    need = rows + 4

    def bev(i):
        k = last - 2 * i
        dy = scal[4 + 2 * k]
        dx = scal[5 + 2 * k]
        base = dy + REACH
        at = i * chans
        inside = (lane + dx >= 0) & (lane + dx < cols)
        turn = jnp.where(dx > 0, cols - dx, -dx)
        for pair in range(need // BEV):
            sides = [
                lifted[pl.ds(base + BEV * pair + half, 3), at : at + chans, :].reshape(3 * chans, cols)
                for half in range(BEV)
            ]
            acc = jnp.dot(w_bev[...], jnp.concatenate(sides, axis=1), preferred_element_type=F32)
            for half in range(BEV):
                row = here * rows - 2 + dy + BEV * pair + half
                value = silu(spread(acc[:, half * cols : (half + 1) * cols], lane, chans))
                value = pltpu.roll(value, turn, 1)
                keep = inside & (row >= 0) & (row < total)
                store(BEV * pair + half, i, jnp.where(keep, value, 0.0).astype(BF))

    for i in range(frames):
        bev(i)


def own_kernel(shape, scal, got, low, mid, high, w_bev, out, ctx, dep, tab, lifted):
    share, chans = shape[1], shape[3]

    def store(j, i, value):
        out[j, i * chans : (i + 1) * chans, :] = value

    lift_and_convolve(
        shape, scal, got, (low, mid, high), w_bev, store, ctx, dep, tab, lifted, 0, 2 * share - 2, share
    )


def join_kernel(
    shape, scal, other, low, mid, high, own, w_bev, far_join, w_out, out, ctx, dep, tab, lifted, moved, hidden, w_join, sem
):
    ranks, share, columns, chans, rows, total, cols, wide = shape
    here = scal[0]
    last = 2 * share - 3
    fetch = pltpu.make_async_copy(far_join, w_join, sem)
    fetch.start()

    def store(j, i, value):
        moved[j, (last - 2 * i) * chans : (last - 2 * i + 1) * chans, :] = value

    lift_and_convolve(
        shape, scal, other, (low, mid, high), w_bev, store, ctx, dep, tab, lifted, scal[2], last, share - 1
    )
    for i in range(share):
        at = (2 * share - 2 - 2 * i) * chans
        for j in range(rows + 4):
            moved[j, at : at + chans, :] = own[j, i * chans : (i + 1) * chans, :]

    fetch.wait()
    lane_wide = lax.broadcasted_iota(jnp.int32, (wide, cols), 1)

    def join(pair, carry):
        acc = None
        for a in range(3):
            both = jnp.concatenate([moved[JOIN * pair + h + a] for h in range(JOIN)], axis=1)
            part = jnp.dot(w_join[a], both, preferred_element_type=F32)
            acc = part if acc is None else acc + part
        for half in range(JOIN):
            row = here * rows - 1 + JOIN * pair + half
            value = silu(spread(acc[:, half * cols : (half + 1) * cols], lane_wide, wide))
            keep = (row >= 0) & (row < total)
            hidden[JOIN * pair + half] = jnp.where(keep, value, 0.0).astype(BF)
        return carry

    lax.fori_loop(0, (rows + 2) // JOIN, join, 0)

    def close(pair, carry):
        sides = [hidden[pl.ds(CLOSE * pair + half, 3), :, :].reshape(3 * wide, cols) for half in range(CLOSE)]
        acc = jnp.dot(w_out[...], jnp.concatenate(sides, axis=1), preferred_element_type=F32)
        for half in range(CLOSE):
            value = spread(acc[:, half * cols : (half + 1) * cols], lane_wide, wide)
            out[CLOSE * pair + half] = value.astype(BF)
        return carry

    lax.fori_loop(0, rows // CLOSE, close, 0)


def taps(weight):
    turned = jnp.transpose(weight, (1, 3, 0, 2))
    return turned.reshape(weight.shape[1] * weight.shape[3], weight.shape[0] * weight.shape[2])


VMEM = pl.BlockSpec(memory_space=pltpu.VMEM)
SMEM = pl.BlockSpec(memory_space=pltpu.SMEM)


def scratch(frames, chans, count, rows, cols):
    span = rows + 2 * EXTRA
    return [
        pltpu.VMEM((frames * chans, count), BF),
        pltpu.VMEM((span, 32, count), F32),
        pltpu.VMEM((3 * rows, cols), jnp.int32),
        pltpu.VMEM((span, frames * chans, cols), BF),
    ]


def call_pack(shape, scal, feats, w_depth, w_ctx):
    ranks, share, columns, chans, rows, total, cols, wide = shape
    return pl.pallas_call(
        functools.partial(pack_kernel, shape),
        out_shape=jax.ShapeDtypeStruct((ranks, share * columns, cols), BF),
        in_specs=[SMEM, VMEM, VMEM, VMEM],
        out_specs=VMEM,
        scratch_shapes=[pltpu.VMEM((share * columns, feats.shape[2]), BF)],
        compiler_params=pltpu.CompilerParams(vmem_limit_bytes=32 * 1024 * 1024),
        name="pack",
    )(scal, feats, w_depth, w_ctx)


def call_own(shape, scal, got, tables, w_bev):
    ranks, share, columns, chans, rows, total, cols, wide = shape
    return pl.pallas_call(
        functools.partial(own_kernel, shape),
        out_shape=jax.ShapeDtypeStruct((rows + 4, share * chans, cols), BF),
        in_specs=[SMEM] + [VMEM] * 5,
        out_specs=VMEM,
        scratch_shapes=scratch(share, chans, ranks * columns, rows, cols),
        compiler_params=pltpu.CompilerParams(vmem_limit_bytes=24 * 1024 * 1024),
        name="own",
    )(scal, got, *tables, w_bev)


def call_join(shape, scal, other, tables, own, w_bev, w_join, w_out):
    ranks, share, columns, chans, rows, total, cols, wide = shape
    return pl.pallas_call(
        functools.partial(join_kernel, shape),
        out_shape=jax.ShapeDtypeStruct((rows, wide, cols), BF),
        in_specs=[SMEM] + [VMEM] * 6 + [pl.BlockSpec(memory_space=pltpu.HBM), VMEM],
        out_specs=VMEM,
        scratch_shapes=scratch(share - 1, chans, ranks * columns, rows, cols)
        + [
            pltpu.VMEM((rows + 4, (2 * share - 1) * chans, cols), BF),
            pltpu.VMEM((rows + 2, wide, cols), BF),
            pltpu.VMEM(w_join.shape, BF),
            pltpu.SemaphoreType.DMA,
        ],
        compiler_params=pltpu.CompilerParams(vmem_limit_bytes=50 * 1024 * 1024),
        name="join",
    )(scal, other, *tables, own, w_bev, w_join, w_out)


def shards(col_feat, w_depth, w_ctx, col_table, w_bev, offsets, w_join, w_out):
    rows, cols = col_table.shape
    frames = offsets.shape[1] + 1
    chans = w_ctx.shape[1]
    wide = w_out.shape[3]
    alone, depth_k = col_feat.shape[1:]
    ranks = lax.axis_size("x") * lax.axis_size("near")
    chips = lax.axis_size("chip")
    total = w_depth.shape[1]
    share = (frames + 1) // 2
    columns = 2 * alone
    shape = (ranks, share, columns, chans, rows, total, cols, wide)
    line = ("x", "far", "near")

    feats = jnp.broadcast_to(col_feat, (chips * 2, alone, depth_k))
    feats = lax.all_to_all(feats, ("chip", "far"), split_axis=0, concat_axis=0, tiled=True)
    w_ctx = jnp.pad(w_ctx, ((0, 0), (0, cols - chans)))
    feats, w_ctx, w_bev, w_out = lax.optimization_barrier((feats, w_ctx, taps(w_bev), taps(w_out)))

    head = jnp.stack(
        [
            lax.axis_index(line).astype(jnp.int32),
            lax.axis_index("chip").astype(jnp.int32) - (share - 1),
            lax.axis_index("core").astype(jnp.int32),
            lax.axis_index("far").astype(jnp.int32),
        ]
    )
    moves = jnp.concatenate([jnp.zeros((1, 2), jnp.int32), offsets[0]], axis=0)
    scal = jnp.concatenate([head, moves.reshape(-1)])

    messages = call_pack(shape, scal, feats, w_depth, w_ctx)
    messages, col_table = lax.optimization_barrier((messages, col_table))
    got = lax.all_to_all(messages, ("x", "near"), split_axis=0, concat_axis=0, tiled=True)
    up = [(i, i + 1) for i in range(2 * ranks - 1)]
    tables = (
        lax.ppermute(col_table, line, up),
        col_table,
        lax.ppermute(col_table, line, [(t, s) for s, t in up]),
    )
    got, tables = lax.optimization_barrier((got, tables))
    other = lax.ppermute(got, "core", [(0, 1), (1, 0)])

    w_join = jnp.transpose(w_join, (0, 1, 3, 2)).reshape(3, 3 * wide, frames * chans)
    own = call_own(shape, scal, got, tables, w_bev)
    joined = call_join(shape, scal, other, tables, own, w_bev, w_join, w_out)
    return joined[None]


def solution(mesh):
    split = Mesh(
        mesh.devices.reshape(mesh.shape["tm"] // 2, 2, mesh.shape["rows"] // 4, 2, 2),
        ("chip", "core", "x", "far", "near"),
    )
    tm, rows = ("chip", "core"), ("x", "far", "near")
    in_specs = (
        P(tm, rows, None),
        P(),
        P(),
        P(rows, None),
        P(),
        P(tm, None, None),
        P(),
        P(),
    )
    out_specs = P(tm, rows, None, None)
    return jax.shard_map(shards, mesh=split, in_specs=in_specs, out_specs=out_specs, check_vma=False)
```

```python
import functools

import jax
import jax.numpy as jnp
from jax import lax
from jax.experimental import pallas as pl
from jax.experimental.pallas import tpu as pltpu
from jax.sharding import Mesh
from jax.sharding import PartitionSpec as P

BF = jnp.bfloat16
F32 = jnp.float32
EXTRA = 7
REACH = 4
GROUP = 3
LIFT = 22
BEV = 2
JOIN = 2
CLOSE = 8


def silu(v):
    return (0.5 * v) * (1.0 + jnp.tanh(0.5 * v))


def spread(acc, lane, chans):
    cols = acc.shape[1]
    low = jnp.where(lane == 0, 0.0, pltpu.roll(acc[:chans], 1, 1))
    high = jnp.where(lane == cols - 1, 0.0, pltpu.roll(acc[2 * chans :], cols - 1, 1))
    return acc[chans : 2 * chans] + low + high


def pack_kernel(shape, scal, feats, w_depth, w_ctx, out, stack):
    ranks, share, columns, chans, rows, total, cols, wide = shape
    span = rows + 2 * EXTRA
    far = scal[3]
    alone = feats.shape[1]
    for slot in range(share):
        source = scal[1] + slot
        for part in range(columns // alone):
            piece = feats[jnp.maximum(source, 0) * (columns // alone) + part]
            at = slot * columns + part * alone
            stack[at : at + alone, :] = jnp.where(source >= 0, piece, jnp.zeros_like(piece))
    stacked = stack[...]
    depth = jax.nn.sigmoid(jnp.dot(stacked, w_depth[...], preferred_element_type=F32))
    main = depth.astype(BF).astype(F32)
    rest = depth - main
    ctx = jnp.dot(stacked, w_ctx[...], preferred_element_type=F32)
    lane = lax.broadcasted_iota(jnp.int32, ctx.shape, 1)
    for rank in range(ranks):
        first = rows * (rank // 2 * 4 + rank % 2 + 2 * far) - EXTRA
        message = jnp.where(lane < chans, ctx, 0.0)
        for part, values in enumerate((main, rest)):
            start = chans + part * span
            turned = pltpu.roll(values, lax.rem(start - first + total, total), 1)
            low = jnp.maximum(start, start - first)
            high = jnp.minimum(start + span, total - first + start)
            message = jnp.where((lane >= low) & (lane < high), turned, message)
        out[rank] = message.astype(BF)


def lift_and_convolve(shape, scal, got, tables, w_bev, store, ctx, dep, tab, lifted, skip, last, frames):
    ranks, share, columns, chans, rows, total, cols, wide = shape
    here = scal[0]
    count = ranks * columns
    span = rows + 2 * EXTRA

    for i in range(frames):
        at = (skip + i) * columns
        if not isinstance(at, int):
            at = pl.multiple_of(at, 16)
        piece = got[:, pl.ds(at, columns), :].reshape(count, cols)
        turned = piece.T.astype(F32)
        ctx[i * chans : (i + 1) * chans, :] = turned[:chans].astype(BF)
        dep[:, i, :] = turned[chans : chans + span]
        dep[:, 16 + i, :] = turned[chans + span : chans + 2 * span]
    for side in range(3):
        tab[side * rows : (side + 1) * rows, :] = tables[side][...]

    alone = columns // 2
    place = lax.broadcasted_iota(jnp.int32, (count, cols), 0)
    number = (place & ~(3 * alone)) | ((place & alone) << 1) | ((place & (2 * alone)) >> 1)

    def lift(pair, carry):
        hots = []
        gains = []
        for half in range(LIFT):
            row = LIFT * pair + half
            seen = tab[pl.ds(row + rows - EXTRA, 1), :]
            hot = jnp.where(number == seen, 1.0, 0.0).astype(BF)
            hots.append(hot)
            both = jnp.dot(dep[row].astype(BF), hot, preferred_element_type=F32)
            gains.append(both[:16] + both[16:])
        hot = jnp.concatenate(hots, axis=1)
        for start in range(0, frames, GROUP):
            stop = min(start + GROUP, frames)
            picked = jnp.dot(
                ctx[start * chans : stop * chans, :], hot, preferred_element_type=F32
            )
            for i in range(start, stop):
                part = picked[(i - start) * chans : (i - start + 1) * chans]
                for half in range(LIFT):
                    value = part[:, half * cols : (half + 1) * cols] * gains[half][i : i + 1, :]
                    lifted[LIFT * pair + half, i * chans : (i + 1) * chans, :] = value.astype(BF)
        return carry

    lax.fori_loop(0, span // LIFT, lift, 0)

    lane = lax.broadcasted_iota(jnp.int32, (chans, cols), 1)
    need = rows + 4

    def bev(i):
        k = last - 2 * i
        dy = scal[4 + 2 * k]
        dx = scal[5 + 2 * k]
        base = dy + REACH
        at = i * chans
        inside = (lane + dx >= 0) & (lane + dx < cols)
        turn = jnp.where(dx > 0, cols - dx, -dx)
        for pair in range(need // BEV):
            sides = [
                lifted[pl.ds(base + BEV * pair + half, 3), at : at + chans, :].reshape(3 * chans, cols)
                for half in range(BEV)
            ]
            acc = jnp.dot(w_bev[...], jnp.concatenate(sides, axis=1), preferred_element_type=F32)
            for half in range(BEV):
                row = here * rows - 2 + dy + BEV * pair + half
                value = silu(spread(acc[:, half * cols : (half + 1) * cols], lane, chans))
                value = pltpu.roll(value, turn, 1)
                keep = inside & (row >= 0) & (row < total)
                store(BEV * pair + half, i, jnp.where(keep, value, 0.0).astype(BF))

    for i in range(frames):
        bev(i)


def own_kernel(shape, scal, got, low, mid, high, w_bev, out, ctx, dep, tab, lifted):
    share, chans = shape[1], shape[3]

    def store(j, i, value):
        out[j, i * chans : (i + 1) * chans, :] = value

    lift_and_convolve(
        shape, scal, got, (low, mid, high), w_bev, store, ctx, dep, tab, lifted, 0, 2 * share - 2, share
    )


def join_kernel(
    shape, scal, other, low, mid, high, own, w_bev, w_join, w_out, out, ctx, dep, tab, lifted, moved, hidden
):
    ranks, share, columns, chans, rows, total, cols, wide = shape
    here = scal[0]
    last = 2 * share - 3

    def store(j, i, value):
        moved[j, (last - 2 * i) * chans : (last - 2 * i + 1) * chans, :] = value

    for i in range(share):
        at = (2 * share - 2 - 2 * i) * chans
        for j in range(rows + 4):
            moved[j, at : at + chans, :] = own[j, i * chans : (i + 1) * chans, :]
    lift_and_convolve(
        shape, scal, other, (low, mid, high), w_bev, store, ctx, dep, tab, lifted, scal[2], last, share - 1
    )

    lane_wide = lax.broadcasted_iota(jnp.int32, (wide, cols), 1)

    def join(pair):
        acc = None
        for a in range(3):
            both = jnp.concatenate([moved[JOIN * pair + h + a] for h in range(JOIN)], axis=1)
            part = jnp.dot(w_join[a], both, preferred_element_type=F32)
            acc = part if acc is None else acc + part
        for half in range(JOIN):
            row = here * rows - 1 + JOIN * pair + half
            value = silu(spread(acc[:, half * cols : (half + 1) * cols], lane_wide, wide))
            keep = (row >= 0) & (row < total)
            hidden[JOIN * pair + half] = jnp.where(keep, value, 0.0).astype(BF)

    for pair in range((rows + 2) // JOIN):
        join(pair)

    def close(pair):
        sides = [hidden[pl.ds(CLOSE * pair + half, 3), :, :].reshape(3 * wide, cols) for half in range(CLOSE)]
        acc = jnp.dot(w_out[...], jnp.concatenate(sides, axis=1), preferred_element_type=F32)
        for half in range(CLOSE):
            value = spread(acc[:, half * cols : (half + 1) * cols], lane_wide, wide)
            out[CLOSE * pair + half] = value.astype(BF)

    for pair in range(rows // CLOSE):
        close(pair)


def taps(weight):
    turned = jnp.transpose(weight, (1, 3, 0, 2))
    return turned.reshape(weight.shape[1] * weight.shape[3], weight.shape[0] * weight.shape[2])


VMEM = pl.BlockSpec(memory_space=pltpu.VMEM)
SMEM = pl.BlockSpec(memory_space=pltpu.SMEM)


def scratch(frames, chans, count, rows, cols):
    span = rows + 2 * EXTRA
    return [
        pltpu.VMEM((frames * chans, count), BF),
        pltpu.VMEM((span, 32, count), F32),
        pltpu.VMEM((3 * rows, cols), jnp.int32),
        pltpu.VMEM((span, frames * chans, cols), BF),
    ]


def call_pack(shape, scal, feats, w_depth, w_ctx):
    ranks, share, columns, chans, rows, total, cols, wide = shape
    return pl.pallas_call(
        functools.partial(pack_kernel, shape),
        out_shape=jax.ShapeDtypeStruct((ranks, share * columns, cols), BF),
        in_specs=[SMEM, VMEM, VMEM, VMEM],
        out_specs=VMEM,
        scratch_shapes=[pltpu.VMEM((share * columns, feats.shape[2]), BF)],
        compiler_params=pltpu.CompilerParams(vmem_limit_bytes=32 * 1024 * 1024),
        name="pack",
    )(scal, feats, w_depth, w_ctx)


def call_own(shape, scal, got, tables, w_bev):
    ranks, share, columns, chans, rows, total, cols, wide = shape
    return pl.pallas_call(
        functools.partial(own_kernel, shape),
        out_shape=jax.ShapeDtypeStruct((rows + 4, share * chans, cols), BF),
        in_specs=[SMEM] + [VMEM] * 5,
        out_specs=VMEM,
        scratch_shapes=scratch(share, chans, ranks * columns, rows, cols),
        compiler_params=pltpu.CompilerParams(vmem_limit_bytes=24 * 1024 * 1024),
        name="own",
    )(scal, got, *tables, w_bev)


def call_join(shape, scal, other, tables, own, w_bev, w_join, w_out):
    ranks, share, columns, chans, rows, total, cols, wide = shape
    return pl.pallas_call(
        functools.partial(join_kernel, shape),
        out_shape=jax.ShapeDtypeStruct((rows, wide, cols), BF),
        in_specs=[SMEM] + [VMEM] * 8,
        out_specs=VMEM,
        scratch_shapes=scratch(share - 1, chans, ranks * columns, rows, cols)
        + [
            pltpu.VMEM((rows + 4, (2 * share - 1) * chans, cols), BF),
            pltpu.VMEM((rows + 2, wide, cols), BF),
        ],
        compiler_params=pltpu.CompilerParams(vmem_limit_bytes=36 * 1024 * 1024),
        name="join",
    )(scal, other, *tables, own, w_bev, w_join, w_out)


def shards(col_feat, w_depth, w_ctx, col_table, w_bev, offsets, w_join, w_out):
    rows, cols = col_table.shape
    frames = offsets.shape[1] + 1
    chans = w_ctx.shape[1]
    wide = w_out.shape[3]
    alone, depth_k = col_feat.shape[1:]
    ranks = lax.axis_size("x") * lax.axis_size("near")
    chips = lax.axis_size("chip")
    total = w_depth.shape[1]
    share = (frames + 1) // 2
    columns = 2 * alone
    shape = (ranks, share, columns, chans, rows, total, cols, wide)
    line = ("x", "far", "near")

    feats = jnp.broadcast_to(col_feat, (chips * 2, alone, depth_k))
    feats = lax.all_to_all(feats, ("chip", "far"), split_axis=0, concat_axis=0, tiled=True)
    w_ctx = jnp.pad(w_ctx, ((0, 0), (0, cols - chans)))
    col_table, w_ctx, w_bev, w_out = lax.optimization_barrier(
        (col_table, w_ctx, taps(w_bev), taps(w_out))
    )
    up = [(i, i + 1) for i in range(2 * ranks - 1)]
    tables = (
        lax.ppermute(col_table, line, up),
        col_table,
        lax.ppermute(col_table, line, [(t, s) for s, t in up]),
    )
    feats, tables, w_ctx, w_bev, w_out = lax.optimization_barrier(
        (feats, tables, w_ctx, w_bev, w_out)
    )

    head = jnp.stack(
        [
            lax.axis_index(line).astype(jnp.int32),
            lax.axis_index("chip").astype(jnp.int32) - (share - 1),
            lax.axis_index("core").astype(jnp.int32),
            lax.axis_index("far").astype(jnp.int32),
        ]
    )
    moves = jnp.concatenate([jnp.zeros((1, 2), jnp.int32), offsets[0]], axis=0)
    scal = jnp.concatenate([head, moves.reshape(-1)])

    messages = call_pack(shape, scal, feats, w_depth, w_ctx)
    got = lax.all_to_all(messages, ("x", "near"), split_axis=0, concat_axis=0, tiled=True)
    other = lax.ppermute(got, "core", [(0, 1), (1, 0)])

    w_join = jnp.transpose(w_join, (0, 1, 3, 2)).reshape(3, 3 * wide, frames * chans)
    own = call_own(shape, scal, got, tables, w_bev)
    joined = call_join(shape, scal, other, tables, own, w_bev, w_join, w_out)
    return joined[None]


def solution(mesh):
    split = Mesh(
        mesh.devices.reshape(mesh.shape["tm"] // 2, 2, mesh.shape["rows"] // 4, 2, 2),
        ("chip", "core", "x", "far", "near"),
    )
    tm, rows = ("chip", "core"), ("x", "far", "near")
    in_specs = (
        P(tm, rows, None),
        P(),
        P(),
        P(rows, None),
        P(),
        P(tm, None, None),
        P(),
        P(),
    )
    out_specs = P(tm, rows, None, None)
    return jax.shard_map(shards, mesh=split, in_specs=in_specs, out_specs=out_specs, check_vma=False)
```

```python
import functools

import jax
import jax.numpy as jnp
from jax import lax
from jax.experimental import pallas as pl
from jax.experimental.pallas import tpu as pltpu
from jax.sharding import Mesh
from jax.sharding import PartitionSpec as P

BF = jnp.bfloat16
F32 = jnp.float32
EXTRA = 7
REACH = 4
GROUP = 3
LIFT = 22
BEV = 2
JOIN = 2
CLOSE = 8


def silu(v):
    return (0.5 * v) * (1.0 + jnp.tanh(0.5 * v))


def spread(acc, lane, chans):
    cols = acc.shape[1]
    low = jnp.where(lane == 0, 0.0, pltpu.roll(acc[:chans], 1, 1))
    high = jnp.where(lane == cols - 1, 0.0, pltpu.roll(acc[2 * chans :], cols - 1, 1))
    return acc[chans : 2 * chans] + low + high


def pack_kernel(shape, scal, feats, w_depth, w_ctx, table, pair_table, out, stack):
    ranks, share, columns, chans, rows, total, cols, wide = shape
    span = rows + 2 * EXTRA
    far = scal[3]
    alone = feats.shape[1]
    for slot in range(share):
        source = scal[1] + slot
        for part in range(columns // alone):
            piece = feats[jnp.maximum(source, 0) * (columns // alone) + part]
            at = slot * columns + part * alone
            stack[at : at + alone, :] = jnp.where(source >= 0, piece, jnp.zeros_like(piece))
    stacked = stack[...]
    depth = jax.nn.sigmoid(jnp.dot(stacked, w_depth[...], preferred_element_type=F32))
    main = depth.astype(BF).astype(F32)
    rest = depth - main
    ctx = jnp.dot(stacked, w_ctx[...], preferred_element_type=F32)
    lane = lax.broadcasted_iota(jnp.int32, ctx.shape, 1)
    mine, theirs = table[...].astype(F32), pair_table[...].astype(F32)
    tabs = jnp.concatenate(
        [jnp.where(far == 0, mine, theirs), jnp.where(far == 0, theirs, mine)], axis=0
    ).astype(BF)
    for rank in range(ranks):
        first = rows * (rank // 2 * 4 + rank % 2 + 2 * far) - EXTRA
        message = jnp.where(lane < chans, ctx, 0.0)
        for part, values in enumerate((main, rest)):
            start = chans + part * span
            turned = pltpu.roll(values, lax.rem(start - first + total, total), 1)
            low = jnp.maximum(start, start - first)
            high = jnp.minimum(start + span, total - first + start)
            message = jnp.where((lane >= low) & (lane < high), turned, message)
        out[rank, : share * columns, :] = message.astype(BF)
        out[rank, share * columns :, :] = tabs


def lift_and_convolve(shape, scal, got, w_bev, store, ctx, dep, tab, lifted, skip, last, frames):
    ranks, share, columns, chans, rows, total, cols, wide = shape
    here = scal[0]
    count = ranks * columns
    span = rows + 2 * EXTRA

    for i in range(frames):
        at = (skip + i) * columns
        if not isinstance(at, int):
            at = pl.multiple_of(at, 16)
        piece = got[:, pl.ds(at, columns), :].reshape(count, cols)
        turned = piece.T.astype(F32)
        ctx[i * chans : (i + 1) * chans, :] = turned[:chans].astype(BF)
        dep[:, i, :] = turned[chans : chans + span]
        dep[:, 16 + i, :] = turned[chans + span : chans + 2 * span]
    for side in range(3):
        block = jnp.clip(here + (side - 1), 0, 2 * ranks - 1)
        both = got[(block >> 2) * 2 + (block & 1), share * columns :, :].astype(F32)
        half = jnp.where((block & 2) == 0, both[:rows], both[rows:])
        tab[side * rows : (side + 1) * rows, :] = half.astype(jnp.int32)

    alone = columns // 2
    place = lax.broadcasted_iota(jnp.int32, (count, cols), 0)
    number = (place & ~(3 * alone)) | ((place & alone) << 1) | ((place & (2 * alone)) >> 1)

    def lift(pair, carry):
        hots = []
        gains = []
        for half in range(LIFT):
            row = LIFT * pair + half
            seen = tab[pl.ds(row + rows - EXTRA, 1), :]
            hot = jnp.where(number == seen, 1.0, 0.0).astype(BF)
            hots.append(hot)
            both = jnp.dot(dep[row].astype(BF), hot, preferred_element_type=F32)
            gains.append(both[:16] + both[16:])
        hot = jnp.concatenate(hots, axis=1)
        for start in range(0, frames, GROUP):
            stop = min(start + GROUP, frames)
            picked = jnp.dot(
                ctx[start * chans : stop * chans, :], hot, preferred_element_type=F32
            )
            for i in range(start, stop):
                part = picked[(i - start) * chans : (i - start + 1) * chans]
                for half in range(LIFT):
                    value = part[:, half * cols : (half + 1) * cols] * gains[half][i : i + 1, :]
                    lifted[LIFT * pair + half, i * chans : (i + 1) * chans, :] = value.astype(BF)
        return carry

    lax.fori_loop(0, span // LIFT, lift, 0)

    lane = lax.broadcasted_iota(jnp.int32, (chans, cols), 1)
    need = rows + 4

    def bev(i):
        k = last - 2 * i
        dy = scal[4 + 2 * k]
        dx = scal[5 + 2 * k]
        base = dy + REACH
        at = i * chans
        inside = (lane + dx >= 0) & (lane + dx < cols)
        turn = jnp.where(dx > 0, cols - dx, -dx)
        for pair in range(need // BEV):
            sides = [
                lifted[pl.ds(base + BEV * pair + half, 3), at : at + chans, :].reshape(3 * chans, cols)
                for half in range(BEV)
            ]
            acc = jnp.dot(w_bev[...], jnp.concatenate(sides, axis=1), preferred_element_type=F32)
            for half in range(BEV):
                row = here * rows - 2 + dy + BEV * pair + half
                value = silu(spread(acc[:, half * cols : (half + 1) * cols], lane, chans))
                value = pltpu.roll(value, turn, 1)
                keep = inside & (row >= 0) & (row < total)
                store(BEV * pair + half, i, jnp.where(keep, value, 0.0).astype(BF))

    for i in range(frames):
        bev(i)


def own_kernel(shape, scal, got, w_bev, out, ctx, dep, tab, lifted):
    share, chans = shape[1], shape[3]

    def store(j, i, value):
        out[j, i * chans : (i + 1) * chans, :] = value

    lift_and_convolve(
        shape, scal, got, w_bev, store, ctx, dep, tab, lifted, 0, 2 * share - 2, share
    )


def join_kernel(
    shape, scal, other, own, w_bev, w_join, w_out, out, ctx, dep, tab, lifted, moved, hidden
):
    ranks, share, columns, chans, rows, total, cols, wide = shape
    here = scal[0]
    last = 2 * share - 3

    def store(j, i, value):
        moved[j, (last - 2 * i) * chans : (last - 2 * i + 1) * chans, :] = value

    for i in range(share):
        at = (2 * share - 2 - 2 * i) * chans
        for j in range(rows + 4):
            moved[j, at : at + chans, :] = own[j, i * chans : (i + 1) * chans, :]
    lift_and_convolve(
        shape, scal, other, w_bev, store, ctx, dep, tab, lifted, scal[2], last, share - 1
    )

    lane_wide = lax.broadcasted_iota(jnp.int32, (wide, cols), 1)

    def join(pair):
        acc = None
        for a in range(3):
            both = jnp.concatenate([moved[JOIN * pair + h + a] for h in range(JOIN)], axis=1)
            part = jnp.dot(w_join[a], both, preferred_element_type=F32)
            acc = part if acc is None else acc + part
        for half in range(JOIN):
            row = here * rows - 1 + JOIN * pair + half
            value = silu(spread(acc[:, half * cols : (half + 1) * cols], lane_wide, wide))
            keep = (row >= 0) & (row < total)
            hidden[JOIN * pair + half] = jnp.where(keep, value, 0.0).astype(BF)

    for pair in range((rows + 2) // JOIN):
        join(pair)

    def close(pair):
        sides = [hidden[pl.ds(CLOSE * pair + half, 3), :, :].reshape(3 * wide, cols) for half in range(CLOSE)]
        acc = jnp.dot(w_out[...], jnp.concatenate(sides, axis=1), preferred_element_type=F32)
        for half in range(CLOSE):
            value = spread(acc[:, half * cols : (half + 1) * cols], lane_wide, wide)
            out[CLOSE * pair + half] = value.astype(BF)

    for pair in range(rows // CLOSE):
        close(pair)


def taps(weight):
    turned = jnp.transpose(weight, (1, 3, 0, 2))
    return turned.reshape(weight.shape[1] * weight.shape[3], weight.shape[0] * weight.shape[2])


VMEM = pl.BlockSpec(memory_space=pltpu.VMEM)
SMEM = pl.BlockSpec(memory_space=pltpu.SMEM)


def scratch(frames, chans, count, rows, cols):
    span = rows + 2 * EXTRA
    return [
        pltpu.VMEM((frames * chans, count), BF),
        pltpu.VMEM((span, 32, count), F32),
        pltpu.VMEM((3 * rows, cols), jnp.int32),
        pltpu.VMEM((span, frames * chans, cols), BF),
    ]


def call_pack(shape, scal, feats, w_depth, w_ctx, table, pair_table):
    ranks, share, columns, chans, rows, total, cols, wide = shape
    return pl.pallas_call(
        functools.partial(pack_kernel, shape),
        out_shape=jax.ShapeDtypeStruct((ranks, share * columns + 2 * rows, cols), BF),
        in_specs=[SMEM] + [VMEM] * 5,
        out_specs=VMEM,
        scratch_shapes=[pltpu.VMEM((share * columns, feats.shape[2]), BF)],
        compiler_params=pltpu.CompilerParams(vmem_limit_bytes=32 * 1024 * 1024),
        name="pack",
    )(scal, feats, w_depth, w_ctx, table, pair_table)


def call_own(shape, scal, got, w_bev):
    ranks, share, columns, chans, rows, total, cols, wide = shape
    return pl.pallas_call(
        functools.partial(own_kernel, shape),
        out_shape=jax.ShapeDtypeStruct((rows + 4, share * chans, cols), BF),
        in_specs=[SMEM] + [VMEM] * 2,
        out_specs=VMEM,
        scratch_shapes=scratch(share, chans, ranks * columns, rows, cols),
        compiler_params=pltpu.CompilerParams(vmem_limit_bytes=24 * 1024 * 1024),
        name="own",
    )(scal, got, w_bev)


def call_join(shape, scal, other, own, w_bev, w_join, w_out):
    ranks, share, columns, chans, rows, total, cols, wide = shape
    return pl.pallas_call(
        functools.partial(join_kernel, shape),
        out_shape=jax.ShapeDtypeStruct((rows, wide, cols), BF),
        in_specs=[SMEM] + [VMEM] * 5,
        out_specs=VMEM,
        scratch_shapes=scratch(share - 1, chans, ranks * columns, rows, cols)
        + [
            pltpu.VMEM((rows + 4, (2 * share - 1) * chans, cols), BF),
            pltpu.VMEM((rows + 2, wide, cols), BF),
        ],
        compiler_params=pltpu.CompilerParams(vmem_limit_bytes=36 * 1024 * 1024),
        name="join",
    )(scal, other, own, w_bev, w_join, w_out)


def shards(col_feat, w_depth, w_ctx, col_table, w_bev, offsets, w_join, w_out):
    rows, cols = col_table.shape
    frames = offsets.shape[1] + 1
    chans = w_ctx.shape[1]
    wide = w_out.shape[3]
    alone, depth_k = col_feat.shape[1:]
    ranks = lax.axis_size("x") * lax.axis_size("near")
    chips = lax.axis_size("chip")
    total = w_depth.shape[1]
    share = (frames + 1) // 2
    columns = 2 * alone
    shape = (ranks, share, columns, chans, rows, total, cols, wide)

    feats = jnp.broadcast_to(col_feat, (chips * 2, alone, depth_k))
    feats = lax.all_to_all(feats, ("chip", "far"), split_axis=0, concat_axis=0, tiled=True)
    pair_table = lax.ppermute(col_table, "far", [(0, 1), (1, 0)])
    w_ctx = jnp.pad(w_ctx, ((0, 0), (0, cols - chans)))
    feats, pair_table, w_ctx, w_bev, w_out = lax.optimization_barrier(
        (feats, pair_table, w_ctx, taps(w_bev), taps(w_out))
    )

    head = jnp.stack(
        [
            lax.axis_index(("x", "far", "near")).astype(jnp.int32),
            lax.axis_index("chip").astype(jnp.int32) - (share - 1),
            lax.axis_index("core").astype(jnp.int32),
            lax.axis_index("far").astype(jnp.int32),
        ]
    )
    moves = jnp.concatenate([jnp.zeros((1, 2), jnp.int32), offsets[0]], axis=0)
    scal = jnp.concatenate([head, moves.reshape(-1)])

    messages = call_pack(shape, scal, feats, w_depth, w_ctx, col_table, pair_table)
    got = lax.all_to_all(messages, ("x", "near"), split_axis=0, concat_axis=0, tiled=True)
    other = lax.ppermute(got, "core", [(0, 1), (1, 0)])

    w_join = jnp.transpose(w_join, (0, 1, 3, 2)).reshape(3, 3 * wide, frames * chans)
    own = call_own(shape, scal, got, w_bev)
    joined = call_join(shape, scal, other, own, w_bev, w_join, w_out)
    return joined[None]


def solution(mesh):
    split = Mesh(
        mesh.devices.reshape(mesh.shape["tm"] // 2, 2, mesh.shape["rows"] // 4, 2, 2),
        ("chip", "core", "x", "far", "near"),
    )
    tm, rows = ("chip", "core"), ("x", "far", "near")
    in_specs = (
        P(tm, rows, None),
        P(),
        P(),
        P(rows, None),
        P(),
        P(tm, None, None),
        P(),
        P(),
    )
    out_specs = P(tm, rows, None, None)
    return jax.shard_map(shards, mesh=split, in_specs=in_specs, out_specs=out_specs, check_vma=False)
```

```python
import functools

import jax
import jax.numpy as jnp
from jax import lax
from jax.experimental import pallas as pl
from jax.experimental.pallas import tpu as pltpu
from jax.sharding import Mesh
from jax.sharding import PartitionSpec as P

BF = jnp.bfloat16
F32 = jnp.float32
EXTRA = 7
REACH = 4
GROUP = 3
LIFT = 22
BEV = 2
JOIN = 2
CLOSE = 8


def silu(v):
    return (0.5 * v) * (1.0 + jnp.tanh(0.5 * v))


def spread(acc, lane, chans):
    cols = acc.shape[1]
    low = jnp.where(lane == 0, 0.0, pltpu.roll(acc[:chans], 1, 1))
    high = jnp.where(lane == cols - 1, 0.0, pltpu.roll(acc[2 * chans :], cols - 1, 1))
    return acc[chans : 2 * chans] + low + high


def pack_kernel(shape, scal, feats, w_depth, w_ctx, table, pair_table, out, stack):
    ranks, share, columns, chans, rows, total, cols, wide = shape
    span = rows + 2 * EXTRA
    far = scal[3]
    alone = feats.shape[1]
    for slot in range(share):
        source = scal[1] + slot
        for part in range(columns // alone):
            piece = feats[jnp.maximum(source, 0) * (columns // alone) + part]
            at = slot * columns + part * alone
            stack[at : at + alone, :] = jnp.where(source >= 0, piece, jnp.zeros_like(piece))
    stacked = stack[...]
    depth = jax.nn.sigmoid(jnp.dot(stacked, w_depth[...], preferred_element_type=F32))
    main = depth.astype(BF).astype(F32)
    rest = depth - main
    turned_ctx = jnp.concatenate(
        [w_ctx[...], jnp.zeros((cols - chans, w_ctx.shape[1]), BF)], axis=0
    )
    ctx = lax.dot_general(stacked, turned_ctx, (((1,), (1,)), ((), ())), preferred_element_type=F32)
    lane = lax.broadcasted_iota(jnp.int32, ctx.shape, 1)
    mine, theirs = table[...].astype(F32), pair_table[...].astype(F32)
    tabs = jnp.concatenate(
        [jnp.where(far == 0, mine, theirs), jnp.where(far == 0, theirs, mine)], axis=0
    ).astype(BF)
    for rank in range(ranks):
        first = rows * (rank // 2 * 4 + rank % 2 + 2 * far) - EXTRA
        message = jnp.where(lane < chans, ctx, 0.0)
        for part, values in enumerate((main, rest)):
            start = chans + part * span
            turned = pltpu.roll(values, lax.rem(start - first + total, total), 1)
            low = jnp.maximum(start, start - first)
            high = jnp.minimum(start + span, total - first + start)
            message = jnp.where((lane >= low) & (lane < high), turned, message)
        out[rank, : share * columns, :] = message.astype(BF)
        out[rank, share * columns :, :] = tabs


def lift_and_convolve(shape, scal, moves, got, w_bev, store, ctx, dep, tab, lifted, skip, last, frames):
    ranks, share, columns, chans, rows, total, cols, wide = shape
    here = scal[0]
    count = ranks * columns
    span = rows + 2 * EXTRA

    for i in range(frames):
        at = (skip + i) * columns
        if not isinstance(at, int):
            at = pl.multiple_of(at, 16)
        piece = got[:, pl.ds(at, columns), :].reshape(count, cols)
        turned = piece.T.astype(F32)
        ctx[i * chans : (i + 1) * chans, :] = turned[:chans].astype(BF)
        dep[:, i, :] = turned[chans : chans + span]
        dep[:, 16 + i, :] = turned[chans + span : chans + 2 * span]
    for side in range(3):
        block = jnp.clip(here + (side - 1), 0, 2 * ranks - 1)
        both = got[(block >> 2) * 2 + (block & 1), share * columns :, :].astype(F32)
        half = jnp.where((block & 2) == 0, both[:rows], both[rows:])
        tab[side * rows : (side + 1) * rows, :] = half.astype(jnp.int32)

    alone = columns // 2
    place = lax.broadcasted_iota(jnp.int32, (count, cols), 0)
    number = (place & ~(3 * alone)) | ((place & alone) << 1) | ((place & (2 * alone)) >> 1)

    def lift(pair, carry):
        hots = []
        gains = []
        for half in range(LIFT):
            row = LIFT * pair + half
            seen = tab[pl.ds(row + rows - EXTRA, 1), :]
            hot = jnp.where(number == seen, 1.0, 0.0).astype(BF)
            hots.append(hot)
            both = jnp.dot(dep[row].astype(BF), hot, preferred_element_type=F32)
            gains.append(both[:16] + both[16:])
        hot = jnp.concatenate(hots, axis=1)
        for start in range(0, frames, GROUP):
            stop = min(start + GROUP, frames)
            picked = jnp.dot(
                ctx[start * chans : stop * chans, :], hot, preferred_element_type=F32
            )
            for i in range(start, stop):
                part = picked[(i - start) * chans : (i - start + 1) * chans]
                for half in range(LIFT):
                    value = part[:, half * cols : (half + 1) * cols] * gains[half][i : i + 1, :]
                    lifted[LIFT * pair + half, i * chans : (i + 1) * chans, :] = value.astype(BF)
        return carry

    lax.fori_loop(0, span // LIFT, lift, 0)

    lane = lax.broadcasted_iota(jnp.int32, (chans, cols), 1)
    need = rows + 4

    def bev(i):
        k = last - 2 * i
        if k == 0:
            dy, dx = jnp.int32(0), jnp.int32(0)
        else:
            dy, dx = moves[0, k - 1], moves[1, k - 1]
        base = dy + REACH
        at = i * chans
        inside = (lane + dx >= 0) & (lane + dx < cols)
        turn = jnp.where(dx > 0, cols - dx, -dx)
        for pair in range(need // BEV):
            sides = [
                lifted[pl.ds(base + BEV * pair + half, 3), at : at + chans, :].reshape(3 * chans, cols)
                for half in range(BEV)
            ]
            acc = jnp.dot(w_bev[...], jnp.concatenate(sides, axis=1), preferred_element_type=F32)
            for half in range(BEV):
                row = here * rows - 2 + dy + BEV * pair + half
                value = silu(spread(acc[:, half * cols : (half + 1) * cols], lane, chans))
                value = pltpu.roll(value, turn, 1)
                keep = inside & (row >= 0) & (row < total)
                store(BEV * pair + half, i, jnp.where(keep, value, 0.0).astype(BF))

    for i in range(frames):
        bev(i)


def turn_taps(weight, out):
    size = weight.shape[3]
    for b in range(3):
        column = jnp.concatenate([weight[a, b] for a in range(3)], axis=0)
        out[b * size : (b + 1) * size, :] = column.astype(F32).T.astype(BF)


def own_kernel(shape, scal, moves, got, weight, out, ctx, dep, tab, lifted, w_bev):
    share, chans = shape[1], shape[3]
    turn_taps(weight, w_bev)

    def store(j, i, value):
        out[j, i * chans : (i + 1) * chans, :] = value

    lift_and_convolve(
        shape, scal, moves, got, w_bev, store, ctx, dep, tab, lifted, 0, 2 * share - 2, share
    )


def join_kernel(
    shape, scal, moves, other, own, weight, w_join, weight_out, out,
    ctx, dep, tab, lifted, moved, hidden, w_bev, w_out,
):
    ranks, share, columns, chans, rows, total, cols, wide = shape
    turn_taps(weight, w_bev)
    turn_taps(weight_out, w_out)
    here = scal[0]
    last = 2 * share - 3

    def store(j, i, value):
        moved[j, (last - 2 * i) * chans : (last - 2 * i + 1) * chans, :] = value

    for i in range(share):
        at = (2 * share - 2 - 2 * i) * chans
        for j in range(rows + 4):
            moved[j, at : at + chans, :] = own[j, i * chans : (i + 1) * chans, :]
    lift_and_convolve(
        shape, scal, moves, other, w_bev, store, ctx, dep, tab, lifted, scal[2], last, share - 1
    )

    lane_wide = lax.broadcasted_iota(jnp.int32, (wide, cols), 1)

    def join(pair):
        acc = None
        for a in range(3):
            both = jnp.concatenate([moved[JOIN * pair + h + a] for h in range(JOIN)], axis=1)
            part = jnp.dot(w_join[a], both, preferred_element_type=F32)
            acc = part if acc is None else acc + part
        for half in range(JOIN):
            row = here * rows - 1 + JOIN * pair + half
            value = silu(spread(acc[:, half * cols : (half + 1) * cols], lane_wide, wide))
            keep = (row >= 0) & (row < total)
            hidden[JOIN * pair + half] = jnp.where(keep, value, 0.0).astype(BF)

    for pair in range((rows + 2) // JOIN):
        join(pair)

    def close(pair):
        sides = [hidden[pl.ds(CLOSE * pair + half, 3), :, :].reshape(3 * wide, cols) for half in range(CLOSE)]
        acc = jnp.dot(w_out[...], jnp.concatenate(sides, axis=1), preferred_element_type=F32)
        for half in range(CLOSE):
            value = spread(acc[:, half * cols : (half + 1) * cols], lane_wide, wide)
            out[CLOSE * pair + half] = value.astype(BF)

    for pair in range(rows // CLOSE):
        close(pair)


VMEM = pl.BlockSpec(memory_space=pltpu.VMEM)
SMEM = pl.BlockSpec(memory_space=pltpu.SMEM)


def scratch(frames, chans, count, rows, cols):
    span = rows + 2 * EXTRA
    return [
        pltpu.VMEM((frames * chans, count), BF),
        pltpu.VMEM((span, 32, count), F32),
        pltpu.VMEM((3 * rows, cols), jnp.int32),
        pltpu.VMEM((span, frames * chans, cols), BF),
    ]


def call_pack(shape, scal, feats, w_depth, w_ctx, table, pair_table):
    ranks, share, columns, chans, rows, total, cols, wide = shape
    return pl.pallas_call(
        functools.partial(pack_kernel, shape),
        out_shape=jax.ShapeDtypeStruct((ranks, share * columns + 2 * rows, cols), BF),
        in_specs=[SMEM] + [VMEM] * 5,
        out_specs=VMEM,
        scratch_shapes=[pltpu.VMEM((share * columns, feats.shape[2]), BF)],
        compiler_params=pltpu.CompilerParams(vmem_limit_bytes=32 * 1024 * 1024),
        name="pack",
    )(scal, feats, w_depth, w_ctx, table, pair_table)


def call_own(shape, scal, moves, got, w_bev):
    ranks, share, columns, chans, rows, total, cols, wide = shape
    return pl.pallas_call(
        functools.partial(own_kernel, shape),
        out_shape=jax.ShapeDtypeStruct((rows + 4, share * chans, cols), BF),
        in_specs=[SMEM] * 2 + [VMEM] * 2,
        out_specs=VMEM,
        scratch_shapes=scratch(share, chans, ranks * columns, rows, cols)
        + [pltpu.VMEM((3 * chans, 3 * chans), BF)],
        compiler_params=pltpu.CompilerParams(vmem_limit_bytes=24 * 1024 * 1024),
        name="own",
    )(scal, moves, got, w_bev)


def call_join(shape, scal, moves, other, own, w_bev, w_join, w_out):
    ranks, share, columns, chans, rows, total, cols, wide = shape
    return pl.pallas_call(
        functools.partial(join_kernel, shape),
        out_shape=jax.ShapeDtypeStruct((rows, wide, cols), BF),
        in_specs=[SMEM] * 2 + [VMEM] * 5,
        out_specs=VMEM,
        scratch_shapes=scratch(share - 1, chans, ranks * columns, rows, cols)
        + [
            pltpu.VMEM((rows + 4, (2 * share - 1) * chans, cols), BF),
            pltpu.VMEM((rows + 2, wide, cols), BF),
            pltpu.VMEM((3 * chans, 3 * chans), BF),
            pltpu.VMEM((3 * wide, 3 * wide), BF),
        ],
        compiler_params=pltpu.CompilerParams(vmem_limit_bytes=36 * 1024 * 1024),
        name="join",
    )(scal, moves, other, own, w_bev, w_join, w_out)


def shards(col_feat, w_depth, w_ctx, col_table, w_bev, offsets, w_join, w_out):
    rows, cols = col_table.shape
    frames = offsets.shape[1] + 1
    chans = w_ctx.shape[1]
    wide = w_out.shape[3]
    alone, depth_k = col_feat.shape[1:]
    ranks = lax.axis_size("x") * lax.axis_size("near")
    chips = lax.axis_size("chip")
    total = w_depth.shape[1]
    share = (frames + 1) // 2
    columns = 2 * alone
    shape = (ranks, share, columns, chans, rows, total, cols, wide)

    feats = jnp.broadcast_to(col_feat, (chips * 2, alone, depth_k))
    feats = lax.all_to_all(feats, ("chip", "far"), split_axis=0, concat_axis=0, tiled=True)
    pair_table = lax.ppermute(col_table, "far", [(0, 1), (1, 0)])
    scal = jnp.stack(
        [
            lax.axis_index(("x", "far", "near")).astype(jnp.int32),
            lax.axis_index("chip").astype(jnp.int32) - (share - 1),
            lax.axis_index("core").astype(jnp.int32),
            lax.axis_index("far").astype(jnp.int32),
        ]
    )
    moves = offsets[0].T

    messages = call_pack(shape, scal, feats, w_depth, w_ctx.T, col_table, pair_table)
    got = lax.all_to_all(messages, ("x", "near"), split_axis=0, concat_axis=0, tiled=True)
    other = lax.ppermute(got, "core", [(0, 1), (1, 0)])

    w_join = jnp.transpose(w_join, (0, 1, 3, 2)).reshape(3, 3 * wide, frames * chans)
    own = call_own(shape, scal, moves, got, w_bev)
    joined = call_join(shape, scal, moves, other, own, w_bev, w_join, w_out)
    return joined[None]


def solution(mesh):
    split = Mesh(
        mesh.devices.reshape(mesh.shape["tm"] // 2, 2, mesh.shape["rows"] // 4, 2, 2),
        ("chip", "core", "x", "far", "near"),
    )
    tm, rows = ("chip", "core"), ("x", "far", "near")
    in_specs = (
        P(tm, rows, None),
        P(),
        P(),
        P(rows, None),
        P(),
        P(tm, None, None),
        P(),
        P(),
    )
    out_specs = P(tm, rows, None, None)
    return jax.shard_map(shards, mesh=split, in_specs=in_specs, out_specs=out_specs, check_vma=False)
```
